256 devices in a mesh: expert: 16 (over z, core), width: 16 (over x, y).
Axes of the slice: x: 4, y: 4, z: 8, core: 2. Of those that a mesh axis runs over, the one named last changes fastest.
Arguments:
- up_weights: float32 [64, 4096, 1536], P('expert', 'width'), may hold values from -0.2 to 0.2
- fisher: float32 [64, 4096], P('expert', 'width'), may hold values from 0.1 to 10
- factor_left: float32 [64, 4096, 128], P('expert', 'width'), may hold values from -0.09375 to 0.09375
- factor_right: float32 [64, 128, 1536], P('expert'), may hold values from -0.25 to 0.25
- calib_rows: bfloat16 [16384, 4096], P('expert', 'width'), may hold values from -6 to 6
- routes: int32 [16384, 1], P('expert'), may hold values from 0 to 63; in each aligned block of 1024 rows (0 to 1023, 1024 to 2047, ...) at most 32 rows name the same one
Outputs:
- shared_base: float32 [4096, 1536], P('width')
- residual_out: float32 [16384, 1536], P('expert', 'width')
The draws below stay inside these ranges and needn't reach their ends.
Inputs may be any that keep to these rules, and one draw needn't show every extreme that they name: `routes`: within the rows of one device (each aligned block of 1024 rows) no expert is named by more than 32 rows, a bound that some block reaches.
All inputs are finite; a program needn't handle non-finite values.
Results may differ from the reference program's by a relative error of at most 0.0003.
Values may be sent and summed in bfloat16 or wider, within the bound.
No kernel may reach another device: no remote copies, remote signals or barrier semaphores. Data moves between devices by JAX's collectives and lax.ppermute only.
A program may use at most 192 MiB of HBM per device.

```python
import math
import jax
import jax.numpy as jnp
import numpy as np
from jax import lax

D = 4096
F = 1536
RANK = 128
TOK_DEV = 1024
EXPERTS = 64
TOKENS = 16384
CAP = 32
N_EXPERT = 16


def draw_up_weights(key, part):
    key_shared = jax.random.fold_in(key, 11)
    key_own = jax.random.fold_in(key, 12)
    shared_part = jax.random.truncated_normal(key_shared, -6.0, 6.0, (1, D, F), jnp.float32)
    own_part = jax.random.truncated_normal(key_own, -6.0, 6.0, (EXPERTS, D, F), jnp.float32)
    return ((shared_part + 0.5 * own_part) * D ** (-0.5)).astype(jnp.float32)


def block_scale(own_key, dims, split, least, top_value):
    level, own = 1.0, jax.random.fold_in(own_key, 6)
    for position, blocks in split:
        steps = jnp.exp(jax.random.uniform(jax.random.fold_in(own, position), (blocks,), jnp.float32, least / len(split), top_value / len(split)))
        level = level * jnp.repeat(steps, dims[position] // blocks).reshape([-1 if axis == position else 1 for axis in range(len(dims))])
    return level


def deal_out(own_key, own, number, rows, number_of, top, reach, slope):
    ranking = jax.random.permutation(own_key, number_of)
    crowded, common = shares(number_of, rows * top, reach, slope, True), shares(number_of, rows * top, reach, slope, False)
    places = jnp.arange(number_of)

    def named(tallies, offset_by):
        used = int((tallies > 0).sum())
        fixed = max(1, used // 4)
        passed = fixed + (places - fixed + offset_by * (used - fixed)) % max(1, number_of - fixed)
        return jnp.zeros((number_of,), jnp.int32).at[ranking[jnp.where(places < fixed, places, passed)]].set(jnp.asarray(tallies, jnp.int32))

    tallies = jnp.where(number % 4 == 0, named(crowded, number // 4), named(common, number - number // 4 - 1))
    mixed = jax.random.permutation(jax.random.fold_in(own, 3), number_of)
    donor, sink = mixed[0:number_of // 2 * 2:2], mixed[1:number_of // 2 * 2:2]
    margin = jnp.minimum(tallies[donor] - 1, reach - tallies[sink]) // 2
    margin = jnp.where((donor == ranking[0]) | (sink == ranking[0]) | (tallies[sink] == 0), 0, jnp.maximum(margin, 0))
    passed = jax.random.randint(jax.random.fold_in(own, 4), (number_of // 2,), 0, 1 << 20) % (margin + 1)
    tallies = tallies.at[donor].add(-passed).at[sink].add(passed)
    labels = jnp.searchsorted(jnp.cumsum(tallies), jnp.arange(rows * top), side="right").astype(jnp.int32)
    grid = labels.reshape(top, rows).T
    grid = grid[jax.random.permutation(jax.random.fold_in(own, 1), rows)]
    offset_by = jax.random.randint(jax.random.fold_in(own, 2), (rows, 1), 0, top)
    return jnp.take_along_axis(grid, (jnp.arange(top)[None, :] + offset_by) % top, axis=1)


def shares(count, total, bound, slope, full):
    portions = [(1 << 20) // math.isqrt(standing ** slope) + 1 for standing in range(1, count + 1)]
    largest = bound if full else min(bound, max(-(-total // count), total * portions[0] // sum(portions)))
    least = 1 if total - largest >= count - 1 else 0
    given, rest = [largest] + [least] * (count - 1), total - largest - least * (count - 1)
    while rest > 0:
        movable = [i for i in range(1, count) if given[i] < largest] or [i for i in range(1, count) if given[i] < bound]
        pool, remaining = sum([portions[i] for i in movable]), rest
        for i in movable:
            addition = min(bound - given[i], max(1, remaining * portions[i] // pool), rest)
            given[i] = given[i] + addition
            rest = rest - addition
    return np.array(given)


def noise(key, shape, deviation, reach, split=(), kind=jnp.bfloat16):
    drawn = deviation * jax.random.normal(key, shape, jnp.float32)
    if split:
        drawn = drawn * block_scale(key, shape, split, -0.22, 0.18)
    return jnp.clip(drawn, -reach, reach).astype(kind)


def setup_inputs(seed: int = 0) -> dict:
    seeds = jax.random.split(jax.random.key(seed), 7)
    up_weights = draw_up_weights(jax.random.fold_in(seeds[6], 71), 0)
    fisher = jnp.clip(jnp.exp(math.log(10.0) - 4.6051702 * jax.random.uniform(seeds[1], (EXPERTS, D), jnp.float32) ** block_scale(seeds[1], (EXPERTS, D), ((0, 16), (1, 16)), -0.2, 0.2)), 0.1, 10.0)
    factor_left = noise(seeds[2], (EXPERTS, D, RANK), D ** -0.5, 0.09375, ((0, 16), (1, 16)), jnp.float32)
    factor_right = noise(seeds[3], (EXPERTS, RANK, F), (4 * RANK) ** -0.5, 0.25, ((0, 16),), jnp.float32)
    calib_rows = noise(seeds[4], (TOKENS, D), 1.0, 6.0, ((0, 16), (1, 16)))
    routes_keys = jax.random.split(jax.random.fold_in(seeds[5], 1), TOKENS // TOK_DEV)
    routes_turns = jax.random.permutation(jax.random.fold_in(seeds[5], 3), TOKENS // TOK_DEV)
    routes = jax.vmap(lambda own, number: deal_out(jax.random.fold_in(seeds[5], 2), own, number, TOK_DEV, EXPERTS, 1, CAP, 2))(routes_keys, routes_turns).reshape((TOKENS, 1))
    return dict(up_weights=up_weights, fisher=fisher, factor_left=factor_left, factor_right=factor_right, calib_rows=calib_rows, routes=routes)


def reference(up_weights, fisher, factor_left, factor_right, calib_rows, routes):
    weight_total = jnp.sum(fisher, axis=0)
    weighted_sum = jnp.einsum("ed,edf->df", fisher, up_weights, precision=lax.Precision.HIGHEST)
    shared_base = weighted_sum / weight_total[:, None]
    route_ids = routes[:, 0]
    most_rows = CAP * N_EXPERT

    def one_expert(accumulated, expert_id):
        chosen_rows = jnp.argsort((route_ids != expert_id).astype(jnp.int32), stable=True)[:most_rows]
        low_rank = jnp.dot(factor_left[expert_id], factor_right[expert_id], precision=lax.Precision.HIGHEST)
        residual = up_weights[expert_id] - shared_base - low_rank
        picked = calib_rows[chosen_rows].astype(jnp.float32)
        product = jnp.dot(picked, residual, precision=lax.Precision.HIGHEST)
        is_live = route_ids[chosen_rows] == expert_id
        accumulated = accumulated.at[chosen_rows].add(jnp.where(is_live[:, None], product, jnp.zeros_like(product)))
        return accumulated, None

    start = jnp.zeros((calib_rows.shape[0], F), jnp.float32)
    result, unused = lax.scan(one_expert, start, jnp.arange(EXPERTS, dtype=jnp.int32))
    return shared_base, result
```

```python
import jax
import jax.numpy as jnp
from jax import lax
from jax.experimental import pallas as pl
from jax.experimental.pallas import tpu as pltpu
from jax.sharding import PartitionSpec as P

f32, bf16, i16, i32 = jnp.float32, jnp.bfloat16, jnp.int16, jnp.int32
VMEM_LIMIT = 48 * 1024 * 1024
TOP = 32000.0
STEPS = 64.0
META = 128


def scale_code(biggest):
    return jnp.ceil(jnp.log2(jnp.maximum(biggest, 2.0**-100)) * STEPS) + 1.0


def up_scale(code):
    return jnp.exp2(code * (-1.0 / STEPS)) * TOP


def down_scale(code):
    return jnp.exp2(code * (1.0 / STEPS)) * (1.0 / TOP)


def to_i16(x):
    return jnp.round(x).astype(i32).astype(i16)


def from_i16(x):
    return x.astype(i32).astype(f32)


def params(*semantics):
    return pltpu.CompilerParams(dimension_semantics=semantics or None, vmem_limit_bytes=VMEM_LIMIT)


def weighted_kernel(up_ref, fisher_ref, out_ref):
    experts, rows, hidden = up_ref.shape
    total = fisher_ref[:, 0:1]
    value = total * up_ref[0]
    for j in range(1, experts):
        level = fisher_ref[:, j : j + 1]
        value = value + level * up_ref[j]
        total = total + level
    code = scale_code(jnp.max(jnp.abs(value), axis=1, keepdims=True))
    coded = to_i16(value * up_scale(code))
    fixed = jnp.round(total * 2.0**20).astype(i32)
    lane = lax.broadcasted_iota(i32, (rows, META), 1)
    meta = jnp.where(lane < 32, code.astype(i32), jnp.where(lane < 64, fixed >> 15, fixed & 32767))
    out_ref[:, :hidden] = coded
    out_ref[:, hidden:] = meta.astype(i16)


def weighted(up_weights, fisher):
    experts, rows, hidden = up_weights.shape
    block = 64
    return pl.pallas_call(
        weighted_kernel,
        grid=(rows // block,),
        in_specs=[
            pl.BlockSpec((experts, block, hidden), lambda i: (0, i, 0)),
            pl.BlockSpec((block, experts), lambda i: (i, 0)),
        ],
        out_specs=pl.BlockSpec((block, hidden + META), lambda i: (i, 0)),
        out_shape=jax.ShapeDtypeStruct((rows, hidden + META), i16),
        compiler_params=params("arbitrary"),
        cost_estimate=pl.CostEstimate(
            flops=2 * up_weights.size, bytes_accessed=4 * up_weights.size, transcendentals=0
        ),
        name="weighted_sum",
    )(up_weights, fisher.T)


def base_kernel(parts_ref, out_ref):
    groups, rows, width = parts_ref.shape
    hidden = width - META
    value = jnp.zeros((rows, hidden), f32)
    total = jnp.zeros((rows, 1), f32)
    for g in range(groups):
        part = from_i16(parts_ref[g])
        value = value + part[:, :hidden] * down_scale(part[:, hidden : hidden + 1])
        total = total + (part[:, hidden + 32 : hidden + 33] * 32768.0 + part[:, hidden + 64 : hidden + 65])
    base = value * (2.0**20 / total)
    code = scale_code(jnp.max(jnp.abs(base), axis=1, keepdims=True))
    out_ref[:, :hidden] = to_i16(base * up_scale(code))
    out_ref[:, hidden:] = jnp.broadcast_to(code.astype(i32), (rows, META)).astype(i16)


def base_slice(parts):
    groups, rows, width = parts.shape
    return pl.pallas_call(
        base_kernel,
        out_shape=jax.ShapeDtypeStruct((rows, width), i16),
        compiler_params=params(),
        name="base_slice",
    )(parts)


def route_kernel(experts, capacity, routes_ref, rows_ref, target_ref, out_ref):
    tokens = rows_ref.shape[0]
    block = out_ref.shape[0]
    step = pl.program_id(0)

    @pl.when(step == 0)
    def _():
        routes = routes_ref[...]
        hit = lax.broadcasted_iota(i32, (experts, tokens), 0) == routes
        one_hot = hit.astype(f32).astype(bf16)
        before = lax.broadcasted_iota(i32, (tokens, tokens), 0) < lax.broadcasted_iota(
            i32, (tokens, tokens), 1
        )
        earlier = jnp.dot(one_hot, before.astype(f32).astype(bf16), preferred_element_type=f32)
        slot = jnp.sum(jnp.where(hit, earlier, 0.0), axis=0, keepdims=True)
        target_ref[...] = routes * capacity + slot.astype(i32)

    place = lax.broadcasted_iota(i32, (block, tokens), 0) + step * block
    chosen = (place == target_ref[...]).astype(f32).astype(bf16)
    out_ref[...] = jnp.dot(chosen, rows_ref[...], preferred_element_type=f32).astype(bf16)


def route(routes, calib_rows, experts, capacity):
    tokens, width = calib_rows.shape
    slots = experts * capacity
    block = 256
    return pl.pallas_call(
        lambda *refs: route_kernel(experts, capacity, *refs),
        grid=(slots // block,),
        in_specs=[
            pl.BlockSpec((1, tokens), lambda i: (0, 0)),
            pl.BlockSpec((tokens, width), lambda i: (0, 0)),
        ],
        out_specs=[
            pl.BlockSpec((1, tokens), lambda i: (0, 0)),
            pl.BlockSpec((block, width), lambda i: (i, 0)),
        ],
        out_shape=[
            jax.ShapeDtypeStruct((1, tokens), i32),
            jax.ShapeDtypeStruct((slots, width), bf16),
        ],
        compiler_params=params("arbitrary"),
        cost_estimate=pl.CostEstimate(
            flops=2 * slots * tokens * width, bytes_accessed=4 * slots * width, transcendentals=0
        ),
        name="route_rows",
    )(routes.reshape(1, tokens), calib_rows)


def product_kernel(coded_ref, up_ref, left_ref, right_ref, rows_ref, base_ref, out_ref):
    width, hidden = base_ref.shape

    @pl.when(pl.program_id(0) == 0)
    def _():
        code = from_i16(coded_ref[:, hidden:])[:, 0:1]
        base_ref[...] = from_i16(coded_ref[:, :hidden]) * down_scale(code)

    groups, _, capacity, _ = rows_ref.shape
    rows = rows_ref[:, 0].reshape(groups * capacity, width)
    contract = (((0,), (1,)), ((), ()))
    block = 384
    for start in range(0, hidden, block):
        part = slice(start, start + block)
        low_rank = jnp.dot(
            left_ref[0], right_ref[0, :, part], precision=lax.Precision.HIGHEST, preferred_element_type=f32
        )
        residual = up_ref[0, :, part] - base_ref[:, part] - low_rank
        high = residual.astype(bf16)
        low = (residual - high.astype(f32)).astype(bf16)
        out_ref[part, :] = lax.dot_general(
            high, rows, contract, preferred_element_type=f32
        ) + lax.dot_general(low, rows, contract, preferred_element_type=f32)


def product(coded_base, up_weights, factor_left, factor_right, routed):
    experts, width, hidden = up_weights.shape
    rank = factor_left.shape[2]
    groups, _, capacity, _ = routed.shape
    rows = groups * capacity
    return pl.pallas_call(
        product_kernel,
        grid=(experts,),
        in_specs=[
            pl.BlockSpec((width, hidden + META), lambda j: (0, 0)),
            pl.BlockSpec((1, width, hidden), lambda j: (j, 0, 0)),
            pl.BlockSpec((1, width, rank), lambda j: (j, 0, 0)),
            pl.BlockSpec((1, rank, hidden), lambda j: (j, 0, 0)),
            pl.BlockSpec((groups, 1, capacity, width), lambda j: (0, j, 0, 0)),
        ],
        out_specs=[
            pl.BlockSpec((width, hidden), lambda j: (0, 0)),
            pl.BlockSpec((hidden, rows), lambda j: (0, j)),
        ],
        out_shape=[
            jax.ShapeDtypeStruct((width, hidden), f32),
            jax.ShapeDtypeStruct((hidden, experts * rows), f32),
        ],
        compiler_params=params("arbitrary"),
        cost_estimate=pl.CostEstimate(
            flops=4 * experts * rows * width * hidden,
            bytes_accessed=4 * (up_weights.size + experts * rows * hidden),
            transcendentals=0,
        ),
        name="routed_product",
    )(coded_base, up_weights, factor_left, factor_right, routed)


def pack_kernel(groups, experts, capacity, values_ref, out_ref):
    columns = values_ref.shape[0]
    span = groups * capacity
    for g in range(groups):
        value = jnp.concatenate(
            [
                values_ref[:, j * span + g * capacity : j * span + (g + 1) * capacity]
                for j in range(experts)
            ],
            axis=1,
        )
        code = scale_code(jnp.max(jnp.abs(value), axis=0, keepdims=True))
        out_ref[g, :columns, :] = to_i16(value * up_scale(code))
        out_ref[g, columns:, :] = jnp.broadcast_to(code.astype(i32), (16, experts * capacity)).astype(i16)


def pack(values, groups, experts, capacity):
    columns = values.shape[0]
    return pl.pallas_call(
        lambda *refs: pack_kernel(groups, experts, capacity, *refs),
        out_shape=jax.ShapeDtypeStruct((groups, columns + 16, experts * capacity), i16),
        compiler_params=params(),
        name="pack_result",
    )(values)


def unpack_kernel(coded_ref, target_ref, out_ref):
    groups, height, slots = coded_ref.shape
    columns, tokens = out_ref.shape
    target = target_ref[...]
    value = jnp.zeros((2 * columns, tokens), f32)
    for g in range(groups):
        part = from_i16(coded_ref[g])
        part = part[:columns] * down_scale(part[columns : columns + 1])
        high = part.astype(bf16)
        low = (part - high.astype(f32)).astype(bf16)
        place = lax.broadcasted_iota(i32, (slots, tokens), 0) + g * slots
        chosen = (place == target).astype(f32).astype(bf16)
        value = value + jnp.dot(
            jnp.concatenate([high, low], axis=0), chosen, preferred_element_type=f32
        )
    out_ref[...] = value[:columns] + value[columns:]


def unpack(coded, target):
    groups, height, slots = coded.shape
    return pl.pallas_call(
        unpack_kernel,
        out_shape=jax.ShapeDtypeStruct((height - 16, target.shape[1]), f32),
        compiler_params=params(),
        name="unpack_result",
    )(coded, target)


def local(up_weights, fisher, factor_left, factor_right, calib_rows, routes):
    exp_local, width_rows, hidden = up_weights.shape
    groups = lax.axis_size("expert")
    expert_total = exp_local * groups
    capacity = 2 * calib_rows.shape[0] // expert_total

    sums = weighted(up_weights, fisher)
    parts = lax.all_to_all(
        sums.reshape(groups, width_rows // groups, hidden + META), "expert", 0, 0, tiled=True
    )
    target, outgoing = route(routes, calib_rows, expert_total, capacity)
    incoming = lax.all_to_all(
        outgoing.reshape(groups, exp_local * capacity, width_rows), "expert", 0, 0, tiled=True
    )
    coded_base = lax.all_gather(base_slice(parts), "expert", tiled=True)
    shared_base, partial_value = product(
        coded_base,
        up_weights,
        factor_left,
        factor_right,
        incoming.reshape(groups, exp_local, capacity, width_rows),
    )
    values = lax.psum_scatter(partial_value, "width", scatter_dimension=0, tiled=True)
    returned = lax.all_to_all(
        pack(values, groups, exp_local, capacity), "expert", 0, 0, tiled=True
    )
    return shared_base, unpack(returned, target).T


def solution(mesh):
    placed = (
        P("expert", "width", None),
        P("expert", "width"),
        P("expert", "width", None),
        P("expert", None, None),
        P("expert", "width"),
        P("expert", None),
    )
    return jax.shard_map(
        local,
        mesh=mesh,
        in_specs=placed,
        out_specs=(P("width", None), P("expert", "width")),
        check_vma=False,
    )
```

```python
import jax
import jax.numpy as jnp
from jax import lax
from jax.experimental import pallas as pl
from jax.experimental.pallas import tpu as pltpu
from jax.sharding import PartitionSpec as P

f32, bf16, i16, i32 = jnp.float32, jnp.bfloat16, jnp.int16, jnp.int32
VMEM_LIMIT = 48 * 1024 * 1024
TOP = 32000.0
STEPS = 64.0
META = 128
SIDE = 4


def scale_code(biggest):
    return jnp.ceil(jnp.log2(jnp.maximum(biggest, 2.0**-100)) * STEPS) + 1.0


def up_scale(code):
    return jnp.exp2(code * (-1.0 / STEPS)) * TOP


def down_scale(code):
    return jnp.exp2(code * (1.0 / STEPS)) * (1.0 / TOP)


def to_i16(x):
    return jnp.round(x).astype(i32).astype(i16)


def from_i16(x):
    return x.astype(i32).astype(f32)


def params(*semantics):
    return pltpu.CompilerParams(dimension_semantics=semantics or None, vmem_limit_bytes=VMEM_LIMIT)


def weighted_kernel(up_ref, fisher_ref, out_ref):
    experts, rows, hidden = up_ref.shape
    total = fisher_ref[:, 0:1]
    value = total * up_ref[0]
    for j in range(1, experts):
        level = fisher_ref[:, j : j + 1]
        value = value + level * up_ref[j]
        total = total + level
    code = scale_code(jnp.max(jnp.abs(value), axis=1, keepdims=True))
    coded = to_i16(value * up_scale(code))
    fixed = jnp.round(total * 2.0**20).astype(i32)
    lane = lax.broadcasted_iota(i32, (rows, META), 1)
    meta = jnp.where(lane < 32, code.astype(i32), jnp.where(lane < 64, fixed >> 15, fixed & 32767))
    out_ref[:, :hidden] = coded
    out_ref[:, hidden:] = meta.astype(i16)


def weighted(up_weights, fisher):
    experts, rows, hidden = up_weights.shape
    block = 64
    return pl.pallas_call(
        weighted_kernel,
        grid=(rows // block,),
        in_specs=[
            pl.BlockSpec((experts, block, hidden), lambda i: (0, i, 0)),
            pl.BlockSpec((block, experts), lambda i: (i, 0)),
        ],
        out_specs=pl.BlockSpec((block, hidden + META), lambda i: (i, 0)),
        out_shape=jax.ShapeDtypeStruct((rows, hidden + META), i16),
        compiler_params=params("arbitrary"),
        cost_estimate=pl.CostEstimate(
            flops=2 * up_weights.size, bytes_accessed=4 * up_weights.size, transcendentals=0
        ),
        name="weighted_sum",
    )(up_weights, fisher.T)


def base_kernel(parts_ref, out_ref):
    groups, rows, width = parts_ref.shape
    hidden = width - META
    value = jnp.zeros((rows, hidden), f32)
    total = jnp.zeros((rows, 1), f32)
    for g in range(groups):
        part = from_i16(parts_ref[g])
        value = value + part[:, :hidden] * down_scale(part[:, hidden : hidden + 1])
        total = total + (part[:, hidden + 32 : hidden + 33] * 32768.0 + part[:, hidden + 64 : hidden + 65])
    base = value * (2.0**20 / total)
    code = scale_code(jnp.max(jnp.abs(base), axis=1, keepdims=True))
    out_ref[:, :hidden] = to_i16(base * up_scale(code))
    out_ref[:, hidden:] = jnp.broadcast_to(code.astype(i32), (rows, META)).astype(i16)


def base_slice(parts):
    groups, rows, width = parts.shape
    return pl.pallas_call(
        base_kernel,
        out_shape=jax.ShapeDtypeStruct((rows, width), i16),
        compiler_params=params(),
        name="base_slice",
    )(parts)


def route_kernel(experts, capacity, routes_ref, rows_ref, target_ref, out_ref):
    tokens = rows_ref.shape[0]
    block = out_ref.shape[0]
    step = pl.program_id(0)

    @pl.when(step == 0)
    def _():
        routes = routes_ref[...]
        hit = lax.broadcasted_iota(i32, (experts, tokens), 0) == routes
        one_hot = hit.astype(f32).astype(bf16)
        before = lax.broadcasted_iota(i32, (tokens, tokens), 0) < lax.broadcasted_iota(
            i32, (tokens, tokens), 1
        )
        earlier = jnp.dot(one_hot, before.astype(f32).astype(bf16), preferred_element_type=f32)
        slot = jnp.sum(jnp.where(hit, earlier, 0.0), axis=0, keepdims=True)
        target_ref[...] = routes * capacity + slot.astype(i32)

    place = lax.broadcasted_iota(i32, (block, tokens), 0) + step * block
    chosen = (place == target_ref[...]).astype(f32).astype(bf16)
    out_ref[...] = jnp.dot(chosen, rows_ref[...], preferred_element_type=f32).astype(bf16)


def route(routes, calib_rows, experts, capacity):
    tokens, width = calib_rows.shape
    slots = experts * capacity
    block = 256
    return pl.pallas_call(
        lambda *refs: route_kernel(experts, capacity, *refs),
        grid=(slots // block,),
        in_specs=[
            pl.BlockSpec((1, tokens), lambda i: (0, 0)),
            pl.BlockSpec((tokens, width), lambda i: (0, 0)),
        ],
        out_specs=[
            pl.BlockSpec((1, tokens), lambda i: (0, 0)),
            pl.BlockSpec((block, width), lambda i: (i, 0)),
        ],
        out_shape=[
            jax.ShapeDtypeStruct((1, tokens), i32),
            jax.ShapeDtypeStruct((slots, width), bf16),
        ],
        compiler_params=params("arbitrary"),
        cost_estimate=pl.CostEstimate(
            flops=2 * slots * tokens * width, bytes_accessed=4 * slots * width, transcendentals=0
        ),
        name="route_rows",
    )(routes.reshape(1, tokens), calib_rows)


def meta_rows(codes):
    lanes = codes[0].shape[1]
    row = lax.broadcasted_iota(i32, (16, lanes), 0)
    meta = jnp.zeros((16, lanes), i32)
    for position, code in enumerate(codes):
        meta = jnp.where(row == position, code.astype(i32), meta)
    return meta.astype(i16)


def encode(value):
    code = scale_code(jnp.max(jnp.abs(value), axis=0, keepdims=True))
    return to_i16(value * up_scale(code)), code


def product_kernel(place_ref, coded_ref, up_ref, left_ref, right_ref, rows_ref, base_ref, *rest):
    side = SIDE
    firsts, seconds, held = rest[:side], rest[side : 2 * side], rest[2 * side]
    width, hidden = base_ref.shape
    block = hidden // side
    columns = block // side
    half = columns // 2

    @pl.when(pl.program_id(0) == 0)
    def _():
        code = from_i16(coded_ref[:, hidden:])[:, 0:1]
        base_ref[...] = from_i16(coded_ref[:, :hidden]) * down_scale(code)

    groups, _, capacity, _ = rows_ref.shape
    rows = rows_ref[:, 0].reshape(groups * capacity, width)
    contract = (((0,), (1,)), ((), ()))
    second_codes = [[] for s in range(side)]
    for r in range(side):
        part = pl.ds(pl.multiple_of(lax.rem(place_ref[0] + r, side) * block, block), block)
        low_rank = jnp.dot(
            left_ref[0], right_ref[0, :, part], precision=lax.Precision.HIGHEST, preferred_element_type=f32
        )
        residual = up_ref[0, :, part] - base_ref[:, part] - low_rank
        high = residual.astype(bf16)
        low = (residual - high.astype(f32)).astype(bf16)
        held[r] = lax.dot_general(high, rows, contract, preferred_element_type=f32) + lax.dot_general(
            low, rows, contract, preferred_element_type=f32
        )
        first_codes = []
        for s in range(side):
            start = lax.rem(place_ref[1] + s, side) * columns
            first = held[r, pl.ds(pl.multiple_of(start, 8), half), :]
            second = held[r, pl.ds(pl.multiple_of(start + half, 8), half), :]
            if r == 0:
                firsts[0][s * half : (s + 1) * half, :] = first
            else:
                coded, code = encode(first)
                firsts[r][s * half : (s + 1) * half, :] = coded
                first_codes.append(code)
            if s == 0:
                seconds[0][r * half : (r + 1) * half, :] = second
            else:
                coded, code = encode(second)
                seconds[s][r * half : (r + 1) * half, :] = coded
                second_codes[s].append(code)
        if r > 0:
            firsts[r][side * half :, :] = meta_rows(first_codes)
    for s in range(1, side):
        seconds[s][side * half :, :] = meta_rows(second_codes[s])


def product(place, coded_base, up_weights, factor_left, factor_right, routed):
    experts, width, hidden = up_weights.shape
    rank = factor_left.shape[2]
    groups, _, capacity, _ = routed.shape
    rows = groups * capacity
    own = hidden // SIDE // 2
    parts = [(own, f32)] + [(own + 16, i16)] * (SIDE - 1)
    return pl.pallas_call(
        product_kernel,
        grid=(experts,),
        in_specs=[
            pl.BlockSpec(memory_space=pltpu.SMEM),
            pl.BlockSpec((width, hidden + META), lambda j: (0, 0)),
            pl.BlockSpec((1, width, hidden), lambda j: (j, 0, 0)),
            pl.BlockSpec((1, width, rank), lambda j: (j, 0, 0)),
            pl.BlockSpec((1, rank, hidden), lambda j: (j, 0, 0)),
            pl.BlockSpec((groups, 1, capacity, width), lambda j: (0, j, 0, 0)),
        ],
        out_specs=[pl.BlockSpec((width, hidden), lambda j: (0, 0))]
        + [pl.BlockSpec((height, rows), lambda j: (0, j)) for height, _ in parts * 2],
        out_shape=[jax.ShapeDtypeStruct((width, hidden), f32)]
        + [jax.ShapeDtypeStruct((height, experts * rows), kind) for height, kind in parts * 2],
        scratch_shapes=[pltpu.VMEM((SIDE, hidden // SIDE, rows), f32)],
        compiler_params=params("arbitrary"),
        cost_estimate=pl.CostEstimate(
            flops=4 * experts * rows * width * hidden,
            bytes_accessed=4 * (up_weights.size + experts * rows * hidden),
            transcendentals=0,
        ),
        name="routed_product",
    )(place, coded_base, up_weights, factor_left, factor_right, routed)


def fold_kernel(*refs):
    side = SIDE
    for which in range(2):
        own, others = refs[which * side], refs[which * side + 1 : (which + 1) * side]
        outs = refs[(2 + which) * side : (3 + which) * side]
        half = own.shape[0] // side
        for s in range(side):
            piece = slice(s * half, (s + 1) * half)
            value = own[piece, :]
            for other in others:
                code = from_i16(other[side * half :, :])[s : s + 1]
                value = value + from_i16(other[piece, :]) * down_scale(code)
            if s == 0:
                outs[0][...] = value
            else:
                coded, code = encode(value)
                outs[s][:half, :] = coded
                outs[s][half:, :] = meta_rows([code])


def fold(firsts, seconds):
    own, total = firsts[0].shape
    half = own // SIDE
    block = 512
    heights = [own] + [own + 16] * (SIDE - 1)
    parts = [(half, f32)] + [(half + 16, i16)] * (SIDE - 1)
    outs = pl.pallas_call(
        fold_kernel,
        grid=(total // block,),
        in_specs=[pl.BlockSpec((height, block), lambda j: (0, j)) for height in heights * 2],
        out_specs=[pl.BlockSpec((height, block), lambda j: (0, j)) for height, _ in parts * 2],
        out_shape=[jax.ShapeDtypeStruct((height, total), kind) for height, kind in parts * 2],
        compiler_params=params("arbitrary"),
        name="fold_sums",
    )(*firsts, *seconds)
    return outs[:SIDE], outs[SIDE:]


def pack_kernel(groups, experts, capacity, *refs):
    side = SIDE
    out_ref = refs[-1]
    halves = []
    for which in range(2):
        own, others = refs[which * side], refs[which * side + 1 : (which + 1) * side]
        half = own.shape[0]
        value = own[...]
        for other in others:
            code = from_i16(other[half:, :])[0:1]
            value = value + from_i16(other[:half, :]) * down_scale(code)
        halves.append(value)
    values = jnp.concatenate(halves, axis=0)
    columns = values.shape[0]
    span = groups * capacity
    for g in range(groups):
        value = jnp.concatenate(
            [values[:, j * span + g * capacity : j * span + (g + 1) * capacity] for j in range(experts)],
            axis=1,
        )
        coded, code = encode(value)
        out_ref[g, :columns, :] = coded
        out_ref[g, columns:, :] = meta_rows([code])


def pack(firsts, seconds, groups, experts, capacity):
    columns = 2 * firsts[0].shape[0]
    return pl.pallas_call(
        lambda *refs: pack_kernel(groups, experts, capacity, *refs),
        out_shape=jax.ShapeDtypeStruct((groups, columns + 16, experts * capacity), i16),
        compiler_params=params(),
        name="pack_result",
    )(*firsts, *seconds)


def step_to(dx, dy):
    side = SIDE
    return [
        (x * side + y, (x + dx) % side * side + (y + dy) % side)
        for x in range(side)
        for y in range(side)
    ]


def exchange(parts, along_x):
    return [parts[0]] + [
        lax.ppermute(parts[r], "width", step_to(r, 0) if along_x else step_to(0, r))
        for r in range(1, SIDE)
    ]


def unpack_kernel(coded_ref, target_ref, out_ref):
    groups, height, slots = coded_ref.shape
    columns, tokens = out_ref.shape
    target = target_ref[...]
    value = jnp.zeros((2 * columns, tokens), f32)
    for g in range(groups):
        part = from_i16(coded_ref[g])
        part = part[:columns] * down_scale(part[columns : columns + 1])
        high = part.astype(bf16)
        low = (part - high.astype(f32)).astype(bf16)
        place = lax.broadcasted_iota(i32, (slots, tokens), 0) + g * slots
        chosen = (place == target).astype(f32).astype(bf16)
        value = value + jnp.dot(
            jnp.concatenate([high, low], axis=0), chosen, preferred_element_type=f32
        )
    out_ref[...] = value[:columns] + value[columns:]


def unpack(coded, target):
    groups, height, slots = coded.shape
    return pl.pallas_call(
        unpack_kernel,
        out_shape=jax.ShapeDtypeStruct((height - 16, target.shape[1]), f32),
        compiler_params=params(),
        name="unpack_result",
    )(coded, target)


def local(up_weights, fisher, factor_left, factor_right, calib_rows, routes):
    exp_local, width_rows, hidden = up_weights.shape
    groups = lax.axis_size("expert")
    expert_total = exp_local * groups
    capacity = 2 * calib_rows.shape[0] // expert_total

    sums = weighted(up_weights, fisher)
    parts = lax.all_to_all(
        sums.reshape(groups, width_rows // groups, hidden + META), "expert", 0, 0, tiled=True
    )
    target, outgoing = route(routes, calib_rows, expert_total, capacity)
    incoming = lax.all_to_all(
        outgoing.reshape(groups, exp_local * capacity, width_rows), "expert", 0, 0, tiled=True
    )
    coded_base = lax.all_gather(base_slice(parts), "expert", tiled=True)
    index = lax.axis_index("width")
    shared_base, *parts = product(
        jnp.stack([index // SIDE, index % SIDE]).astype(i32),
        coded_base,
        up_weights,
        factor_left,
        factor_right,
        incoming.reshape(groups, exp_local, capacity, width_rows),
    )
    firsts, seconds = fold(exchange(parts[:SIDE], True), exchange(parts[SIDE:], False))
    values = pack(exchange(firsts, False), exchange(seconds, True), groups, exp_local, capacity)
    returned = lax.all_to_all(values, "expert", 0, 0, tiled=True)
    return shared_base, unpack(returned, target).T


def solution(mesh):
    placed = (
        P("expert", "width", None),
        P("expert", "width"),
        P("expert", "width", None),
        P("expert", None, None),
        P("expert", "width"),
        P("expert", None),
    )
    return jax.shard_map(
        local,
        mesh=mesh,
        in_specs=placed,
        out_specs=(P("width", None), P("expert", "width")),
        check_vma=False,
    )
```

```python
import jax
import jax.numpy as jnp
from jax import lax
from jax.experimental import pallas as pl
from jax.experimental.pallas import tpu as pltpu
from jax.sharding import PartitionSpec as P

f32, bf16, i16, i32 = jnp.float32, jnp.bfloat16, jnp.int16, jnp.int32
VMEM_LIMIT = 48 * 1024 * 1024
TOP = 32000.0
STEPS = 64.0
META = 128
SIDE = 4


def scale_code(biggest):
    return jnp.ceil(jnp.log2(jnp.maximum(biggest, 2.0**-100)) * STEPS) + 1.0


def up_scale(code):
    return jnp.exp2(code * (-1.0 / STEPS)) * TOP


def down_scale(code):
    return jnp.exp2(code * (1.0 / STEPS)) * (1.0 / TOP)


def to_i16(x):
    return jnp.round(x).astype(i32).astype(i16)


def from_i16(x):
    return x.astype(i32).astype(f32)


def params(*semantics):
    return pltpu.CompilerParams(dimension_semantics=semantics or None, vmem_limit_bytes=VMEM_LIMIT)


def weighted_kernel(up_ref, fisher_ref, out_ref):
    experts, rows, hidden = up_ref.shape
    total = fisher_ref[:, 0:1]
    value = total * up_ref[0]
    for j in range(1, experts):
        level = fisher_ref[:, j : j + 1]
        value = value + level * up_ref[j]
        total = total + level
    code = scale_code(jnp.max(jnp.abs(value), axis=1, keepdims=True))
    coded = to_i16(value * up_scale(code))
    fixed = jnp.round(total * 2.0**20).astype(i32)
    lane = lax.broadcasted_iota(i32, (rows, META), 1)
    meta = jnp.where(lane < 32, code.astype(i32), jnp.where(lane < 64, fixed >> 15, fixed & 32767))
    out_ref[:, :hidden] = coded
    out_ref[:, hidden:] = meta.astype(i16)


def weighted(up_weights, fisher):
    experts, rows, hidden = up_weights.shape
    block = 64
    return pl.pallas_call(
        weighted_kernel,
        grid=(rows // block,),
        in_specs=[
            pl.BlockSpec((experts, block, hidden), lambda i: (0, i, 0)),
            pl.BlockSpec((block, experts), lambda i: (i, 0)),
        ],
        out_specs=pl.BlockSpec((block, hidden + META), lambda i: (i, 0)),
        out_shape=jax.ShapeDtypeStruct((rows, hidden + META), i16),
        compiler_params=params("arbitrary"),
        cost_estimate=pl.CostEstimate(
            flops=2 * up_weights.size, bytes_accessed=4 * up_weights.size, transcendentals=0
        ),
        name="weighted_sum",
    )(up_weights, fisher.T)


def base_kernel(place_ref, parts_ref, out_ref):
    groups, rows, width = parts_ref.shape
    hidden = width - META
    value = jnp.zeros((rows, hidden), f32)
    total = jnp.zeros((rows, 1), f32)
    for g in range(groups):
        part = from_i16(parts_ref[g])
        value = value + part[:, :hidden] * down_scale(part[:, hidden : hidden + 1])
        total = total + (part[:, hidden + 32 : hidden + 33] * 32768.0 + part[:, hidden + 64 : hidden + 65])
    base = value * (2.0**20 / total)
    code = scale_code(jnp.max(jnp.abs(base), axis=1, keepdims=True))
    coded = to_i16(base * up_scale(code))
    meta = jnp.broadcast_to(code.astype(i32), (rows, META)).astype(i16)
    block = hidden // SIDE
    for x in range(SIDE):
        start = pl.multiple_of(lax.rem(x - place_ref[0] + SIDE, SIDE) * (block + META), META)
        out_ref[:, pl.ds(start, block)] = coded[:, x * block : (x + 1) * block]
        out_ref[:, pl.ds(pl.multiple_of(start + block, META), META)] = meta


def base_slice(place, parts):
    groups, rows, width = parts.shape
    return pl.pallas_call(
        base_kernel,
        in_specs=[pl.BlockSpec(memory_space=pltpu.SMEM), pl.BlockSpec(memory_space=pltpu.VMEM)],
        out_shape=jax.ShapeDtypeStruct((rows, width - META + SIDE * META), i16),
        compiler_params=params(),
        name="base_slice",
    )(place, parts)


def route_kernel(experts, capacity, routes_ref, rows_ref, target_ref, out_ref):
    tokens = rows_ref.shape[0]
    block = out_ref.shape[0]
    step = pl.program_id(0)

    @pl.when(step == 0)
    def _():
        routes = routes_ref[...]
        hit = lax.broadcasted_iota(i32, (experts, tokens), 0) == routes
        one_hot = hit.astype(f32).astype(bf16)
        before = lax.broadcasted_iota(i32, (tokens, tokens), 0) < lax.broadcasted_iota(
            i32, (tokens, tokens), 1
        )
        earlier = jnp.dot(one_hot, before.astype(f32).astype(bf16), preferred_element_type=f32)
        slot = jnp.sum(jnp.where(hit, earlier, 0.0), axis=0, keepdims=True)
        target_ref[...] = routes * capacity + slot.astype(i32)

    place = lax.broadcasted_iota(i32, (block, tokens), 0) + step * block
    chosen = (place == target_ref[...]).astype(f32).astype(bf16)
    out_ref[...] = jnp.dot(chosen, rows_ref[...], preferred_element_type=f32).astype(bf16)


def route(routes, calib_rows, experts, capacity):
    tokens, width = calib_rows.shape
    slots = experts * capacity
    block = 256
    return pl.pallas_call(
        lambda *refs: route_kernel(experts, capacity, *refs),
        grid=(slots // block,),
        in_specs=[
            pl.BlockSpec((1, tokens), lambda i: (0, 0)),
            pl.BlockSpec((tokens, width), lambda i: (0, 0)),
        ],
        out_specs=[
            pl.BlockSpec((1, tokens), lambda i: (0, 0)),
            pl.BlockSpec((block, width), lambda i: (i, 0)),
        ],
        out_shape=[
            jax.ShapeDtypeStruct((1, tokens), i32),
            jax.ShapeDtypeStruct((slots, width), bf16),
        ],
        compiler_params=params("arbitrary"),
        cost_estimate=pl.CostEstimate(
            flops=2 * slots * tokens * width, bytes_accessed=4 * slots * width, transcendentals=0
        ),
        name="route_rows",
    )(routes.reshape(1, tokens), calib_rows)


def meta_rows(codes):
    lanes = codes[0].shape[1]
    row = lax.broadcasted_iota(i32, (16, lanes), 0)
    meta = jnp.zeros((16, lanes), i32)
    for position, code in enumerate(codes):
        meta = jnp.where(row == position, code.astype(i32), meta)
    return meta.astype(i16)


def split(value):
    high = value.astype(bf16)
    return high, (value - high.astype(f32)).astype(bf16)


def encode(value):
    code = scale_code(jnp.max(jnp.abs(value), axis=0, keepdims=True))
    return to_i16(value * up_scale(code)), code


def product_kernel(place_ref, up_ref, left_ref, right_ref, rows_ref, *rest):
    side = SIDE
    firsts, seconds, held = rest[:side], rest[side : 2 * side], rest[2 * side]
    _, width, hidden = up_ref.shape
    block = hidden // side
    columns = block // side
    half = columns // 2

    groups, _, capacity, _ = rows_ref.shape
    rows = rows_ref[:, 0].reshape(groups * capacity, width)
    contract = (((0,), (1,)), ((), ()))
    second_codes = [[] for s in range(side)]
    left_high, left_low = split(left_ref[0])
    left_all = jnp.concatenate([left_high, left_low], axis=1)
    for r in range(side):
        part = pl.ds(pl.multiple_of(lax.rem(place_ref[0] + r, side) * block, block), block)
        right_high, right_low = split(right_ref[0, :, part])
        low_rank = jnp.dot(
            left_all, jnp.concatenate([right_high] * 2, axis=0), preferred_element_type=f32
        ) + jnp.dot(left_high, right_low, preferred_element_type=f32)
        high, low = split(up_ref[0, :, part] - low_rank)
        held[r] = lax.dot_general(high, rows, contract, preferred_element_type=f32) + lax.dot_general(
            low, rows, contract, preferred_element_type=f32
        )
        first_codes = []
        for s in range(side):
            start = lax.rem(place_ref[1] + s, side) * columns
            first = held[r, pl.ds(pl.multiple_of(start, 8), half), :]
            second = held[r, pl.ds(pl.multiple_of(start + half, 8), half), :]
            if r == 0:
                firsts[0][s * half : (s + 1) * half, :] = first
            else:
                coded, code = encode(first)
                firsts[r][s * half : (s + 1) * half, :] = coded
                first_codes.append(code)
            if s == 0:
                seconds[0][r * half : (r + 1) * half, :] = second
            else:
                coded, code = encode(second)
                seconds[s][r * half : (r + 1) * half, :] = coded
                second_codes[s].append(code)
        if r > 0:
            firsts[r][side * half :, :] = meta_rows(first_codes)
    for s in range(1, side):
        seconds[s][side * half :, :] = meta_rows(second_codes[s])


def product(place, up_weights, factor_left, factor_right, routed):
    experts, width, hidden = up_weights.shape
    rank = factor_left.shape[2]
    groups, _, capacity, _ = routed.shape
    rows = groups * capacity
    own = hidden // SIDE // 2
    parts = [(own, f32)] + [(own + 16, i16)] * (SIDE - 1)
    return pl.pallas_call(
        product_kernel,
        grid=(experts,),
        in_specs=[
            pl.BlockSpec(memory_space=pltpu.SMEM),
            pl.BlockSpec((1, width, hidden), lambda j: (j, 0, 0)),
            pl.BlockSpec((1, width, rank), lambda j: (j, 0, 0)),
            pl.BlockSpec((1, rank, hidden), lambda j: (j, 0, 0)),
            pl.BlockSpec((groups, 1, capacity, width), lambda j: (0, j, 0, 0)),
        ],
        out_specs=[pl.BlockSpec((height, rows), lambda j: (0, j)) for height, _ in parts * 2],
        out_shape=[jax.ShapeDtypeStruct((height, experts * rows), kind) for height, kind in parts * 2],
        scratch_shapes=[pltpu.VMEM((SIDE, hidden // SIDE, rows), f32)],
        compiler_params=params("arbitrary"),
        cost_estimate=pl.CostEstimate(
            flops=4 * experts * rows * width * hidden,
            bytes_accessed=4 * (up_weights.size + experts * rows * hidden),
            transcendentals=0,
        ),
        name="routed_product",
    )(place, up_weights, factor_left, factor_right, routed)


def base_product_kernel(place_ref, *refs):
    side = SIDE
    full, codeds, rows = refs[0], refs[1:side], refs[side : 2 * side]
    base_ref, outs = refs[2 * side], refs[2 * side + 1 : 3 * side + 1]
    held = refs[-1]
    hidden = base_ref.shape[1]
    block = hidden // side
    columns = block // side
    scale = down_scale(from_i16(full[:, block : block + META])[:, 0:1])
    for x in range(side):
        start = lax.rem(x - place_ref[0] + side, side) * (block + META)
        base_ref[:, x * block : (x + 1) * block] = (
            from_i16(full[:, pl.ds(pl.multiple_of(start, META), block)]) * scale
        )
    contract = (((0,), (1,)), ((), ()))
    value = None
    for r in range(side):
        coded = full if r == 0 else codeds[r - 1]
        part = from_i16(coded[:, :block]) * down_scale(from_i16(coded[:, block : block + META])[:, 0:1])
        for term in split(part):
            added = lax.dot_general(term, rows[r][...], contract, preferred_element_type=f32)
            value = added if value is None else value + added
    held[...] = value
    for s in range(side):
        start = pl.multiple_of(lax.rem(place_ref[1] + s, side) * columns, 8)
        piece = held[pl.ds(start, columns), :]
        if s == 0:
            outs[0][...] = piece
        else:
            coded, code = encode(piece)
            outs[s][:columns, :] = coded
            outs[s][columns:, :] = meta_rows([code])


def base_product(place, full, codeds, rows):
    width = full.shape[0]
    tokens = rows[0].shape[0]
    hidden = full.shape[1] - SIDE * META
    columns = hidden // SIDE // SIDE
    vmem = pl.BlockSpec(memory_space=pltpu.VMEM)
    outs = pl.pallas_call(
        base_product_kernel,
        in_specs=[pl.BlockSpec(memory_space=pltpu.SMEM)] + [vmem] * (2 * SIDE),
        out_shape=[
            jax.ShapeDtypeStruct((width, hidden), f32),
            jax.ShapeDtypeStruct((columns, tokens), f32),
        ]
        + [jax.ShapeDtypeStruct((columns + 16, tokens), i16)] * (SIDE - 1),
        scratch_shapes=[pltpu.VMEM((hidden // SIDE, tokens), f32)],
        compiler_params=params(),
        cost_estimate=pl.CostEstimate(
            flops=4 * width * tokens * hidden, bytes_accessed=8 * width * hidden, transcendentals=0
        ),
        name="base_product",
    )(place, full, *codeds, *rows)
    return outs[0], outs[1:]


def fold_kernel(*refs):
    side = SIDE
    for which in range(2):
        own, others = refs[which * side], refs[which * side + 1 : (which + 1) * side]
        outs = refs[(2 + which) * side : (3 + which) * side]
        half = own.shape[0] // side
        for s in range(side):
            piece = slice(s * half, (s + 1) * half)
            value = own[piece, :]
            for other in others:
                code = from_i16(other[side * half :, :])[s : s + 1]
                value = value + from_i16(other[piece, :]) * down_scale(code)
            if s == 0:
                outs[0][...] = value
            else:
                coded, code = encode(value)
                outs[s][:half, :] = coded
                outs[s][half:, :] = meta_rows([code])


def fold(firsts, seconds):
    own, total = firsts[0].shape
    half = own // SIDE
    block = 512
    heights = [own] + [own + 16] * (SIDE - 1)
    parts = [(half, f32)] + [(half + 16, i16)] * (SIDE - 1)
    outs = pl.pallas_call(
        fold_kernel,
        grid=(total // block,),
        in_specs=[pl.BlockSpec((height, block), lambda j: (0, j)) for height in heights * 2],
        out_specs=[pl.BlockSpec((height, block), lambda j: (0, j)) for height, _ in parts * 2],
        out_shape=[jax.ShapeDtypeStruct((height, total), kind) for height, kind in parts * 2],
        compiler_params=params("arbitrary"),
        name="fold_sums",
    )(*firsts, *seconds)
    return outs[:SIDE], outs[SIDE:]


def pack_kernel(groups, experts, capacity, *refs):
    side = SIDE
    out_ref = refs[-1]
    halves = []
    for which in range(2):
        own, others = refs[which * side], refs[which * side + 1 : (which + 1) * side]
        half = own.shape[0]
        value = own[...]
        for other in others:
            code = from_i16(other[half:, :])[0:1]
            value = value + from_i16(other[:half, :]) * down_scale(code)
        halves.append(value)
    values = jnp.concatenate(halves, axis=0)
    columns = values.shape[0]
    span = groups * capacity
    for g in range(groups):
        value = jnp.concatenate(
            [values[:, j * span + g * capacity : j * span + (g + 1) * capacity] for j in range(experts)],
            axis=1,
        )
        coded, code = encode(value)
        out_ref[g, :columns, :] = coded
        out_ref[g, columns:, :] = meta_rows([code])


def pack(firsts, seconds, groups, experts, capacity):
    columns = 2 * firsts[0].shape[0]
    return pl.pallas_call(
        lambda *refs: pack_kernel(groups, experts, capacity, *refs),
        out_shape=jax.ShapeDtypeStruct((groups, columns + 16, experts * capacity), i16),
        compiler_params=params(),
        name="pack_result",
    )(*firsts, *seconds)


def step_to(dx, dy):
    side = SIDE
    return [
        (x * side + y, (x + dx) % side * side + (y + dy) % side)
        for x in range(side)
        for y in range(side)
    ]


def exchange(parts, along_x):
    return [parts[0]] + [
        lax.ppermute(parts[r], "width", step_to(r, 0) if along_x else step_to(0, r))
        for r in range(1, SIDE)
    ]


def unpack_kernel(coded_ref, target_ref, *rest):
    own, others, out_ref = rest[0], rest[1:SIDE], rest[SIDE]
    groups, height, slots = coded_ref.shape
    columns, tokens = out_ref.shape
    target = target_ref[...]
    value = jnp.zeros((2 * columns, tokens), f32)
    for g in range(groups):
        part = from_i16(coded_ref[g])
        terms = split(part[:columns] * down_scale(part[columns : columns + 1]))
        place = lax.broadcasted_iota(i32, (slots, tokens), 0) + g * slots
        chosen = (place == target).astype(f32).astype(bf16)
        value = value + jnp.dot(jnp.concatenate(terms, axis=0), chosen, preferred_element_type=f32)
    base = own[...]
    for other in others:
        base = base + from_i16(other[:columns, :]) * down_scale(from_i16(other[columns:, :])[0:1])
    out_ref[...] = value[:columns] + value[columns:] - base


def unpack(coded, target, base_parts):
    groups, height, slots = coded.shape
    return pl.pallas_call(
        unpack_kernel,
        out_shape=jax.ShapeDtypeStruct((height - 16, target.shape[1]), f32),
        compiler_params=params(),
        name="unpack_result",
    )(coded, target, *base_parts)


def local(up_weights, fisher, factor_left, factor_right, calib_rows, routes):
    exp_local, width_rows, hidden = up_weights.shape
    groups = lax.axis_size("expert")
    expert_total = exp_local * groups
    capacity = 2 * calib_rows.shape[0] // expert_total

    index = lax.axis_index("width")
    place = jnp.stack([index // SIDE, index % SIDE]).astype(i32)

    rows_along_x = exchange([calib_rows] * SIDE, True)
    target, outgoing = route(routes, calib_rows, expert_total, capacity)
    incoming = lax.all_to_all(
        outgoing.reshape(groups, exp_local * capacity, width_rows), "expert", 0, 0, tiled=True
    )
    sums = weighted(up_weights, fisher)
    incoming, sums, rows_along_x = lax.optimization_barrier((incoming, sums, rows_along_x))
    parts = product(
        place,
        up_weights,
        factor_left,
        factor_right,
        incoming.reshape(groups, exp_local, capacity, width_rows),
    )
    sums = lax.all_to_all(
        sums.reshape(groups, width_rows // groups, hidden + META), "expert", 0, 0, tiled=True
    )
    firsts, seconds = exchange(parts[:SIDE], True), exchange(parts[SIDE:], False)
    coded_base = base_slice(place, sums)
    coded_base, firsts[1], seconds[1] = lax.optimization_barrier((coded_base, firsts[1], seconds[1]))
    coded_base = lax.all_gather(coded_base, "expert", tiled=True)
    coded_base, firsts, seconds = lax.optimization_barrier((coded_base, firsts, seconds))
    span = hidden // SIDE + META
    chunks = exchange([coded_base[:, r * span : (r + 1) * span] for r in range(SIDE)], True)
    firsts, seconds = fold(firsts, seconds)
    firsts, seconds = exchange(firsts, False), exchange(seconds, True)
    chunks, firsts, seconds = lax.optimization_barrier((chunks, firsts, seconds))
    values = pack(firsts, seconds, groups, exp_local, capacity)
    shared_base, base_parts = base_product(place, coded_base, chunks[1:], rows_along_x)
    base_parts = exchange(base_parts, False)
    returned = lax.all_to_all(values, "expert", 0, 0, tiled=True)
    return shared_base, unpack(returned, target, base_parts).T


def solution(mesh):
    placed = (
        P("expert", "width", None),
        P("expert", "width"),
        P("expert", "width", None),
        P("expert", None, None),
        P("expert", "width"),
        P("expert", None),
    )
    return jax.shard_map(
        local,
        mesh=mesh,
        in_specs=placed,
        out_specs=(P("width", None), P("expert", "width")),
        check_vma=False,
    )
```

```python
import jax
import jax.numpy as jnp
from jax import lax
from jax.experimental import pallas as pl
from jax.experimental.pallas import tpu as pltpu
from jax.sharding import PartitionSpec as P

f32, bf16, i16, i32 = jnp.float32, jnp.bfloat16, jnp.int16, jnp.int32
VMEM_LIMIT = 48 * 1024 * 1024
TOP = 32000.0
STEPS = 64.0
META = 128
SIDE = 4


def scale_code(biggest):
    return jnp.ceil(jnp.log2(jnp.maximum(biggest, 2.0**-100)) * STEPS) + 1.0


def up_scale(code):
    return jnp.exp2(code * (-1.0 / STEPS)) * TOP


def down_scale(code):
    return jnp.exp2(code * (1.0 / STEPS)) * (1.0 / TOP)


def to_i16(x):
    return jnp.round(x).astype(i32).astype(i16)


def from_i16(x):
    return x.astype(i32).astype(f32)


def params(*semantics):
    return pltpu.CompilerParams(dimension_semantics=semantics or None, vmem_limit_bytes=VMEM_LIMIT)


def weighted_kernel(place_ref, up_ref, fisher_ref, *outs):
    experts, rows, hidden = up_ref.shape
    block = hidden // SIDE
    total = fisher_ref[:, 0:1]
    for j in range(1, experts):
        total = total + fisher_ref[:, j : j + 1]
    fixed = jnp.round(total * 2.0**20).astype(i32)
    lane = lax.broadcasted_iota(i32, (rows, META), 1)
    fixed = jnp.where(lane < 64, fixed >> 15, fixed & 32767)
    for r in range(SIDE):
        part = pl.ds(pl.multiple_of(lax.rem(place_ref[0] + r, SIDE) * block, META), block)
        value = fisher_ref[:, 0:1] * up_ref[0, :, part]
        for j in range(1, experts):
            value = value + fisher_ref[:, j : j + 1] * up_ref[j, :, part]
        code = scale_code(jnp.max(jnp.abs(value), axis=1, keepdims=True))
        outs[r][:, :block] = to_i16(value * up_scale(code))
        outs[r][:, block:] = jnp.where(lane < 32, code.astype(i32), fixed).astype(i16)


def weighted(place, up_weights, fisher):
    experts, rows, hidden = up_weights.shape
    block = 64
    width = hidden // SIDE + META
    return pl.pallas_call(
        weighted_kernel,
        grid=(rows // block,),
        in_specs=[
            pl.BlockSpec(memory_space=pltpu.SMEM),
            pl.BlockSpec((experts, block, hidden), lambda i: (0, i, 0)),
            pl.BlockSpec((block, experts), lambda i: (i, 0)),
        ],
        out_specs=[pl.BlockSpec((block, width), lambda i: (i, 0))] * SIDE,
        out_shape=[jax.ShapeDtypeStruct((rows, width), i16)] * SIDE,
        compiler_params=params("arbitrary"),
        cost_estimate=pl.CostEstimate(
            flops=2 * up_weights.size, bytes_accessed=4 * up_weights.size, transcendentals=0
        ),
        name="weighted_sum",
    )(place, up_weights, fisher.T)


def base_kernel(parts_ref, out_ref):
    groups, rows, width = parts_ref.shape
    hidden = width - META
    value = jnp.zeros((rows, hidden), f32)
    total = jnp.zeros((rows, 1), f32)
    for g in range(groups):
        part = from_i16(parts_ref[g])
        value = value + part[:, :hidden] * down_scale(part[:, hidden : hidden + 1])
        total = total + (part[:, hidden + 32 : hidden + 33] * 32768.0 + part[:, hidden + 64 : hidden + 65])
    base = value * (2.0**20 / total)
    code = scale_code(jnp.max(jnp.abs(base), axis=1, keepdims=True))
    out_ref[:, :hidden] = to_i16(base * up_scale(code))
    out_ref[:, hidden:] = jnp.broadcast_to(code.astype(i32), (rows, META)).astype(i16)


def base_slice(parts):
    groups, rows, width = parts.shape
    return pl.pallas_call(
        base_kernel,
        out_shape=jax.ShapeDtypeStruct((rows, width), i16),
        compiler_params=params(),
        name="base_slice",
    )(parts)


def decode_rows(coded):
    block = coded.shape[1] - META
    return from_i16(coded[:, :block]) * down_scale(from_i16(coded[:, block:])[:, 0:1])


def shared_kernel(place_ref, *refs):
    out_ref = refs[-1]
    block = out_ref.shape[1] // SIDE
    for r in range(SIDE):
        start = pl.multiple_of(lax.rem(place_ref[0] + r, SIDE) * block, META)
        out_ref[:, pl.ds(start, block)] = decode_rows(refs[r][...])


def shared(place, codeds):
    rows, width = codeds[0].shape
    vmem = pl.BlockSpec(memory_space=pltpu.VMEM)
    return pl.pallas_call(
        shared_kernel,
        in_specs=[pl.BlockSpec(memory_space=pltpu.SMEM)] + [vmem] * SIDE,
        out_shape=jax.ShapeDtypeStruct((rows, (width - META) * SIDE), f32),
        compiler_params=params(),
        name="shared_base",
    )(place, *codeds)


def route_kernel(experts, capacity, routes_ref, rows_ref, target_ref, out_ref):
    tokens = rows_ref.shape[0]
    block = out_ref.shape[0]
    step = pl.program_id(0)

    @pl.when(step == 0)
    def _():
        routes = routes_ref[...]
        hit = lax.broadcasted_iota(i32, (experts, tokens), 0) == routes
        one_hot = hit.astype(f32).astype(bf16)
        before = lax.broadcasted_iota(i32, (tokens, tokens), 0) < lax.broadcasted_iota(
            i32, (tokens, tokens), 1
        )
        earlier = jnp.dot(one_hot, before.astype(f32).astype(bf16), preferred_element_type=f32)
        slot = jnp.sum(jnp.where(hit, earlier, 0.0), axis=0, keepdims=True)
        target_ref[...] = routes * capacity + slot.astype(i32)

    place = lax.broadcasted_iota(i32, (block, tokens), 0) + step * block
    chosen = (place == target_ref[...]).astype(f32).astype(bf16)
    out_ref[...] = jnp.dot(chosen, rows_ref[...], preferred_element_type=f32).astype(bf16)


def route(routes, calib_rows, experts, capacity):
    tokens, width = calib_rows.shape
    slots = experts * capacity
    block = 256
    return pl.pallas_call(
        lambda *refs: route_kernel(experts, capacity, *refs),
        grid=(slots // block,),
        in_specs=[
            pl.BlockSpec((1, tokens), lambda i: (0, 0)),
            pl.BlockSpec((tokens, width), lambda i: (0, 0)),
        ],
        out_specs=[
            pl.BlockSpec((1, tokens), lambda i: (0, 0)),
            pl.BlockSpec((block, width), lambda i: (i, 0)),
        ],
        out_shape=[
            jax.ShapeDtypeStruct((1, tokens), i32),
            jax.ShapeDtypeStruct((slots, width), bf16),
        ],
        compiler_params=params("arbitrary"),
        cost_estimate=pl.CostEstimate(
            flops=2 * slots * tokens * width, bytes_accessed=4 * slots * width, transcendentals=0
        ),
        name="route_rows",
    )(routes.reshape(1, tokens), calib_rows)


def meta_rows(codes):
    lanes = codes[0].shape[1]
    row = lax.broadcasted_iota(i32, (16, lanes), 0)
    meta = jnp.zeros((16, lanes), i32)
    for position, code in enumerate(codes):
        meta = jnp.where(row == position, code.astype(i32), meta)
    return meta.astype(i16)


def split(value):
    high = value.astype(bf16)
    return high, (value - high.astype(f32)).astype(bf16)


def encode(value):
    code = scale_code(jnp.max(jnp.abs(value), axis=0, keepdims=True))
    return to_i16(value * up_scale(code)), code


def product_kernel(place_ref, up_ref, left_ref, right_ref, rows_ref, *rest):
    side = SIDE
    firsts, seconds, held = rest[:side], rest[side : 2 * side], rest[2 * side]
    _, width, hidden = up_ref.shape
    block = hidden // side
    columns = block // side
    half = columns // 2

    groups, _, capacity, _ = rows_ref.shape
    rows = rows_ref[:, 0].reshape(groups * capacity, width)
    contract = (((0,), (1,)), ((), ()))
    second_codes = [[] for s in range(side)]
    left_high, left_low = split(left_ref[0])
    left_all = jnp.concatenate([left_high, left_low], axis=1)
    for r in range(side):
        part = pl.ds(pl.multiple_of(lax.rem(place_ref[0] + r, side) * block, block), block)
        right_high, right_low = split(right_ref[0, :, part])
        low_rank = jnp.dot(
            left_all, jnp.concatenate([right_high] * 2, axis=0), preferred_element_type=f32
        ) + jnp.dot(left_high, right_low, preferred_element_type=f32)
        high, low = split(up_ref[0, :, part] - low_rank)
        held[r] = lax.dot_general(high, rows, contract, preferred_element_type=f32) + lax.dot_general(
            low, rows, contract, preferred_element_type=f32
        )
        first_codes = []
        for s in range(side):
            start = lax.rem(place_ref[1] + s, side) * columns
            first = held[r, pl.ds(pl.multiple_of(start, 8), half), :]
            second = held[r, pl.ds(pl.multiple_of(start + half, 8), half), :]
            if r == 0:
                firsts[0][s * half : (s + 1) * half, :] = first
            else:
                coded, code = encode(first)
                firsts[r][s * half : (s + 1) * half, :] = coded
                first_codes.append(code)
            if s == 0:
                seconds[0][r * half : (r + 1) * half, :] = second
            else:
                coded, code = encode(second)
                seconds[s][r * half : (r + 1) * half, :] = coded
                second_codes[s].append(code)
        if r > 0:
            firsts[r][side * half :, :] = meta_rows(first_codes)
    for s in range(1, side):
        seconds[s][side * half :, :] = meta_rows(second_codes[s])


def product(place, up_weights, factor_left, factor_right, routed):
    experts, width, hidden = up_weights.shape
    rank = factor_left.shape[2]
    groups, _, capacity, _ = routed.shape
    rows = groups * capacity
    own = hidden // SIDE // 2
    parts = [(own, f32)] + [(own + 16, i16)] * (SIDE - 1)
    return pl.pallas_call(
        product_kernel,
        grid=(experts,),
        in_specs=[
            pl.BlockSpec(memory_space=pltpu.SMEM),
            pl.BlockSpec((1, width, hidden), lambda j: (j, 0, 0)),
            pl.BlockSpec((1, width, rank), lambda j: (j, 0, 0)),
            pl.BlockSpec((1, rank, hidden), lambda j: (j, 0, 0)),
            pl.BlockSpec((groups, 1, capacity, width), lambda j: (0, j, 0, 0)),
        ],
        out_specs=[pl.BlockSpec((height, rows), lambda j: (0, j)) for height, _ in parts * 2],
        out_shape=[jax.ShapeDtypeStruct((height, experts * rows), kind) for height, kind in parts * 2],
        scratch_shapes=[pltpu.VMEM((SIDE, hidden // SIDE, rows), f32)],
        compiler_params=params("arbitrary"),
        cost_estimate=pl.CostEstimate(
            flops=4 * experts * rows * width * hidden,
            bytes_accessed=4 * (up_weights.size + experts * rows * hidden),
            transcendentals=0,
        ),
        name="routed_product",
    )(place, up_weights, factor_left, factor_right, routed)


def base_product_kernel(place_ref, coded_ref, *refs):
    side = SIDE
    rows, outs, held = refs[:side], refs[side : 2 * side], refs[-1]
    groups, _, height, width = coded_ref.shape
    columns = held.shape[0] // side
    contract = (((0,), (1,)), ((), ()))
    value = None
    for r in range(side):
        part = decode_rows(coded_ref[:, r].reshape(groups * height, width))
        for term in split(part):
            added = lax.dot_general(term, rows[r][...], contract, preferred_element_type=f32)
            value = added if value is None else value + added
    held[...] = value
    for s in range(side):
        start = pl.multiple_of(lax.rem(place_ref[1] + s, side) * columns, 8)
        piece = held[pl.ds(start, columns), :]
        if s == 0:
            outs[0][...] = piece
        else:
            coded, code = encode(piece)
            outs[s][:columns, :] = coded
            outs[s][columns:, :] = meta_rows([code])


def base_product(place, coded, rows):
    groups, side, height, width = coded.shape
    tokens = rows[0].shape[0]
    block = width - META
    columns = block // side
    vmem = pl.BlockSpec(memory_space=pltpu.VMEM)
    return pl.pallas_call(
        base_product_kernel,
        in_specs=[pl.BlockSpec(memory_space=pltpu.SMEM)] + [vmem] * (side + 1),
        out_shape=[jax.ShapeDtypeStruct((columns, tokens), f32)]
        + [jax.ShapeDtypeStruct((columns + 16, tokens), i16)] * (side - 1),
        scratch_shapes=[pltpu.VMEM((block, tokens), f32)],
        compiler_params=params(),
        cost_estimate=pl.CostEstimate(
            flops=4 * groups * side * height * tokens * block,
            bytes_accessed=4 * groups * side * height * block,
            transcendentals=0,
        ),
        name="base_product",
    )(place, coded, *rows)


def fold_kernel(*refs):
    side = SIDE
    for which in range(2):
        own, others = refs[which * side], refs[which * side + 1 : (which + 1) * side]
        outs = refs[(2 + which) * side : (3 + which) * side]
        half = own.shape[0] // side
        for s in range(side):
            piece = slice(s * half, (s + 1) * half)
            value = own[piece, :]
            for other in others:
                code = from_i16(other[side * half :, :])[s : s + 1]
                value = value + from_i16(other[piece, :]) * down_scale(code)
            if s == 0:
                outs[0][...] = value
            else:
                coded, code = encode(value)
                outs[s][:half, :] = coded
                outs[s][half:, :] = meta_rows([code])


def fold(firsts, seconds):
    own, total = firsts[0].shape
    half = own // SIDE
    block = 512
    heights = [own] + [own + 16] * (SIDE - 1)
    parts = [(half, f32)] + [(half + 16, i16)] * (SIDE - 1)
    outs = pl.pallas_call(
        fold_kernel,
        grid=(total // block,),
        in_specs=[pl.BlockSpec((height, block), lambda j: (0, j)) for height in heights * 2],
        out_specs=[pl.BlockSpec((height, block), lambda j: (0, j)) for height, _ in parts * 2],
        out_shape=[jax.ShapeDtypeStruct((height, total), kind) for height, kind in parts * 2],
        compiler_params=params("arbitrary"),
        name="fold_sums",
    )(*firsts, *seconds)
    return outs[:SIDE], outs[SIDE:]


def pack_kernel(groups, experts, capacity, *refs):
    side = SIDE
    out_ref = refs[-1]
    halves = []
    for which in range(2):
        own, others = refs[which * side], refs[which * side + 1 : (which + 1) * side]
        half = own.shape[0]
        value = own[...]
        for other in others:
            code = from_i16(other[half:, :])[0:1]
            value = value + from_i16(other[:half, :]) * down_scale(code)
        halves.append(value)
    values = jnp.concatenate(halves, axis=0)
    columns = values.shape[0]
    span = groups * capacity
    for g in range(groups):
        value = jnp.concatenate(
            [values[:, j * span + g * capacity : j * span + (g + 1) * capacity] for j in range(experts)],
            axis=1,
        )
        coded, code = encode(value)
        out_ref[g, :columns, :] = coded
        out_ref[g, columns:, :] = meta_rows([code])


def pack(firsts, seconds, groups, experts, capacity):
    columns = 2 * firsts[0].shape[0]
    return pl.pallas_call(
        lambda *refs: pack_kernel(groups, experts, capacity, *refs),
        out_shape=jax.ShapeDtypeStruct((groups, columns + 16, experts * capacity), i16),
        compiler_params=params(),
        name="pack_result",
    )(*firsts, *seconds)


def step_to(dx, dy):
    side = SIDE
    return [
        (x * side + y, (x + dx) % side * side + (y + dy) % side)
        for x in range(side)
        for y in range(side)
    ]


def exchange(parts, along_x, sign=1):
    return [parts[0]] + [
        lax.ppermute(parts[r], "width", step_to(sign * r, 0) if along_x else step_to(0, sign * r))
        for r in range(1, SIDE)
    ]


def unpack_kernel(coded_ref, target_ref, *rest):
    own, others, out_ref = rest[0], rest[1:SIDE], rest[SIDE]
    groups, height, slots = coded_ref.shape
    columns, tokens = out_ref.shape
    target = target_ref[...]
    value = jnp.zeros((2 * columns, tokens), f32)
    for g in range(groups):
        part = from_i16(coded_ref[g])
        terms = split(part[:columns] * down_scale(part[columns : columns + 1]))
        place = lax.broadcasted_iota(i32, (slots, tokens), 0) + g * slots
        chosen = (place == target).astype(f32).astype(bf16)
        value = value + jnp.dot(jnp.concatenate(terms, axis=0), chosen, preferred_element_type=f32)
    base = own[...]
    for other in others:
        base = base + from_i16(other[:columns, :]) * down_scale(from_i16(other[columns:, :])[0:1])
    out_ref[...] = value[:columns] + value[columns:] - base


def unpack(coded, target, base_parts):
    groups, height, slots = coded.shape
    return pl.pallas_call(
        unpack_kernel,
        out_shape=jax.ShapeDtypeStruct((height - 16, target.shape[1]), f32),
        compiler_params=params(),
        name="unpack_result",
    )(coded, target, *base_parts)


def local(up_weights, fisher, factor_left, factor_right, calib_rows, routes):
    exp_local, width_rows, hidden = up_weights.shape
    groups = lax.axis_size("expert")
    expert_total = exp_local * groups
    capacity = 2 * calib_rows.shape[0] // expert_total

    index = lax.axis_index("width")
    place = jnp.stack([index // SIDE, index % SIDE]).astype(i32)

    rows_along_x = exchange([calib_rows] * SIDE, True)
    target, outgoing = route(routes, calib_rows, expert_total, capacity)
    incoming = lax.all_to_all(
        outgoing.reshape(groups, exp_local * capacity, width_rows), "expert", 0, 0, tiled=True
    )
    sums = exchange(weighted(place, up_weights, fisher), True)
    incoming, sums = lax.optimization_barrier((incoming, sums))
    parts = product(
        place,
        up_weights,
        factor_left,
        factor_right,
        incoming.reshape(groups, exp_local, capacity, width_rows),
    )
    parts, rows_along_x = lax.optimization_barrier((parts, rows_along_x))
    height, span = width_rows // groups, hidden // SIDE + META
    sums = jnp.stack([part.reshape(groups, height, span) for part in sums], axis=1)
    sums = lax.all_to_all(
        sums.reshape(groups, SIDE * height, span), "expert", 0, 0, tiled=True
    )
    firsts, seconds = exchange(parts[:SIDE], True), exchange(parts[SIDE:], False)
    coded_base = base_slice(sums)
    coded_base, firsts[1] = lax.optimization_barrier((coded_base, firsts[1]))
    coded_base = lax.all_gather(coded_base, "expert", tiled=True)
    coded_base = coded_base.reshape(groups, SIDE, height, span)
    coded_base, firsts, seconds = lax.optimization_barrier((coded_base, firsts, seconds))
    firsts, seconds = fold(firsts, seconds)
    base_parts = exchange(base_product(place, coded_base, rows_along_x), False)
    firsts, seconds = exchange(firsts, False), exchange(seconds, True)
    values = pack(firsts, seconds, groups, exp_local, capacity)
    returned = lax.all_to_all(values, "expert", 0, 0, tiled=True)
    chunks = [coded_base[:, r].reshape(width_rows, span) for r in range(SIDE)]
    shared_base = shared(place, exchange(chunks, True, -1))
    return shared_base, unpack(returned, target, base_parts).T


def solution(mesh):
    placed = (
        P("expert", "width", None),
        P("expert", "width"),
        P("expert", "width", None),
        P("expert", None, None),
        P("expert", "width"),
        P("expert", None),
    )
    return jax.shard_map(
        local,
        mesh=mesh,
        in_specs=placed,
        out_specs=(P("width", None), P("expert", "width")),
        check_vma=False,
    )
```

```python
import jax
import jax.numpy as jnp
from jax import lax
from jax.experimental import pallas as pl
from jax.experimental.pallas import tpu as pltpu
from jax.sharding import PartitionSpec as P

f32, bf16, i16, i32 = jnp.float32, jnp.bfloat16, jnp.int16, jnp.int32
VMEM_LIMIT = 48 * 1024 * 1024
TOP = 32000.0
STEPS = 64.0
META = 128
SIDE = 4


def scale_code(biggest):
    return jnp.ceil(jnp.log2(jnp.maximum(biggest, 2.0**-100)) * STEPS) + 1.0


def up_scale(code):
    return jnp.exp2(code * (-1.0 / STEPS)) * TOP


def down_scale(code):
    return jnp.exp2(code * (1.0 / STEPS)) * (1.0 / TOP)


def to_i16(x):
    return jnp.round(x).astype(i32).astype(i16)


def from_i16(x):
    return x.astype(i32).astype(f32)


def params(*semantics):
    return pltpu.CompilerParams(dimension_semantics=semantics or None, vmem_limit_bytes=VMEM_LIMIT)


def weighted_kernel(place_ref, up_ref, fisher_ref, *outs):
    experts, rows, hidden = up_ref.shape
    block = hidden // SIDE
    total = fisher_ref[:, 0:1]
    for j in range(1, experts):
        total = total + fisher_ref[:, j : j + 1]
    fixed = jnp.round(total * 2.0**20).astype(i32)
    lane = lax.broadcasted_iota(i32, (rows, META), 1)
    fixed = jnp.where(lane < 64, fixed >> 15, fixed & 32767)
    for r in range(SIDE):
        part = pl.ds(pl.multiple_of(lax.rem(place_ref[0] + r, SIDE) * block, META), block)
        value = fisher_ref[:, 0:1] * up_ref[0, :, part]
        for j in range(1, experts):
            value = value + fisher_ref[:, j : j + 1] * up_ref[j, :, part]
        code = scale_code(jnp.max(jnp.abs(value), axis=1, keepdims=True))
        outs[r][:, :block] = to_i16(value * up_scale(code))
        outs[r][:, block:] = jnp.where(lane < 32, code.astype(i32), fixed).astype(i16)


def weighted(place, up_weights, fisher):
    experts, rows, hidden = up_weights.shape
    block = 64
    width = hidden // SIDE + META
    return pl.pallas_call(
        weighted_kernel,
        grid=(rows // block,),
        in_specs=[
            pl.BlockSpec(memory_space=pltpu.SMEM),
            pl.BlockSpec((experts, block, hidden), lambda i: (0, i, 0)),
            pl.BlockSpec((block, experts), lambda i: (i, 0)),
        ],
        out_specs=[pl.BlockSpec((block, width), lambda i: (i, 0))] * SIDE,
        out_shape=[jax.ShapeDtypeStruct((rows, width), i16)] * SIDE,
        compiler_params=params("arbitrary"),
        cost_estimate=pl.CostEstimate(
            flops=2 * up_weights.size, bytes_accessed=4 * up_weights.size, transcendentals=0
        ),
        name="weighted_sum",
    )(place, up_weights, fisher.T)


def base_kernel(parts_ref, out_ref):
    groups, rows, width = parts_ref.shape
    hidden = width - META
    value = jnp.zeros((rows, hidden), f32)
    total = jnp.zeros((rows, 1), f32)
    for g in range(groups):
        part = from_i16(parts_ref[g])
        value = value + part[:, :hidden] * down_scale(part[:, hidden : hidden + 1])
        total = total + (part[:, hidden + 32 : hidden + 33] * 32768.0 + part[:, hidden + 64 : hidden + 65])
    base = value * (2.0**20 / total)
    code = scale_code(jnp.max(jnp.abs(base), axis=1, keepdims=True))
    out_ref[:, :hidden] = to_i16(base * up_scale(code))
    out_ref[:, hidden:] = jnp.broadcast_to(code.astype(i32), (rows, META)).astype(i16)


def base_slice(parts):
    groups, rows, width = parts.shape
    return pl.pallas_call(
        base_kernel,
        out_shape=jax.ShapeDtypeStruct((rows, width), i16),
        compiler_params=params(),
        name="base_slice",
    )(parts)


def decode_rows(coded):
    block = coded.shape[1] - META
    return from_i16(coded[:, :block]) * down_scale(from_i16(coded[:, block:])[:, 0:1])


def shared_kernel(place_ref, *refs):
    out_ref = refs[-1]
    block = out_ref.shape[1] // SIDE
    for r in range(SIDE):
        start = pl.multiple_of(lax.rem(place_ref[0] + r, SIDE) * block, META)
        out_ref[:, pl.ds(start, block)] = decode_rows(refs[r][...])


def shared(place, codeds):
    rows, width = codeds[0].shape
    vmem = pl.BlockSpec(memory_space=pltpu.VMEM)
    return pl.pallas_call(
        shared_kernel,
        in_specs=[pl.BlockSpec(memory_space=pltpu.SMEM)] + [vmem] * SIDE,
        out_shape=jax.ShapeDtypeStruct((rows, (width - META) * SIDE), f32),
        compiler_params=params(),
        name="shared_base",
    )(place, *codeds)


def route_kernel(experts, capacity, routes_ref, rows_ref, target_ref, out_ref):
    tokens = rows_ref.shape[0]
    block = out_ref.shape[0]
    step = pl.program_id(0)

    @pl.when(step == 0)
    def _():
        routes = routes_ref[...]
        hit = lax.broadcasted_iota(i32, (experts, tokens), 0) == routes
        one_hot = hit.astype(f32).astype(bf16)
        before = lax.broadcasted_iota(i32, (tokens, tokens), 0) < lax.broadcasted_iota(
            i32, (tokens, tokens), 1
        )
        earlier = jnp.dot(one_hot, before.astype(f32).astype(bf16), preferred_element_type=f32)
        slot = jnp.sum(jnp.where(hit, earlier, 0.0), axis=0, keepdims=True)
        target_ref[...] = routes * capacity + slot.astype(i32)

    place = lax.broadcasted_iota(i32, (block, tokens), 0) + step * block
    chosen = (place == target_ref[...]).astype(f32).astype(bf16)
    out_ref[...] = jnp.dot(chosen, rows_ref[...], preferred_element_type=f32).astype(bf16)


def route(routes, calib_rows, experts, capacity):
    tokens, width = calib_rows.shape
    slots = experts * capacity
    block = 256
    return pl.pallas_call(
        lambda *refs: route_kernel(experts, capacity, *refs),
        grid=(slots // block,),
        in_specs=[
            pl.BlockSpec((1, tokens), lambda i: (0, 0)),
            pl.BlockSpec((tokens, width), lambda i: (0, 0)),
        ],
        out_specs=[
            pl.BlockSpec((1, tokens), lambda i: (0, 0)),
            pl.BlockSpec((block, width), lambda i: (i, 0)),
        ],
        out_shape=[
            jax.ShapeDtypeStruct((1, tokens), i32),
            jax.ShapeDtypeStruct((slots, width), bf16),
        ],
        compiler_params=params("arbitrary"),
        cost_estimate=pl.CostEstimate(
            flops=2 * slots * tokens * width, bytes_accessed=4 * slots * width, transcendentals=0
        ),
        name="route_rows",
    )(routes.reshape(1, tokens), calib_rows)


def meta_rows(codes):
    lanes = codes[0].shape[1]
    row = lax.broadcasted_iota(i32, (16, lanes), 0)
    meta = jnp.zeros((16, lanes), i32)
    for position, code in enumerate(codes):
        meta = jnp.where(row == position, code.astype(i32), meta)
    return meta.astype(i16)


def split(value):
    high = value.astype(bf16)
    return high, (value - high.astype(f32)).astype(bf16)


def encode(value):
    code = scale_code(jnp.max(jnp.abs(value), axis=0, keepdims=True))
    return to_i16(value * up_scale(code)), code


def product_kernel(place_ref, up_ref, left_ref, right_ref, rows_ref, *rest):
    side = SIDE
    firsts, seconds, held = rest[:side], rest[side : 2 * side], rest[2 * side]
    _, width, hidden = up_ref.shape
    block = hidden // side
    columns = block // side
    half = columns // 2

    groups, _, capacity, _ = rows_ref.shape
    rows = rows_ref[:, 0].reshape(groups * capacity, width)
    contract = (((0,), (1,)), ((), ()))
    second_codes = [[] for s in range(side)]
    left_high, left_low = split(left_ref[0])
    left_all = jnp.concatenate([left_high, left_low], axis=1)
    for r in range(side):
        part = pl.ds(pl.multiple_of(lax.rem(place_ref[0] + r, side) * block, block), block)
        right_high, right_low = split(right_ref[0, :, part])
        low_rank = jnp.dot(
            left_all, jnp.concatenate([right_high] * 2, axis=0), preferred_element_type=f32
        ) + jnp.dot(left_high, right_low, preferred_element_type=f32)
        high, low = split(up_ref[0, :, part] - low_rank)
        held[r] = lax.dot_general(high, rows, contract, preferred_element_type=f32) + lax.dot_general(
            low, rows, contract, preferred_element_type=f32
        )
        first_codes = []
        for s in range(side):
            start = lax.rem(place_ref[1] + s, side) * columns
            first = held[r, pl.ds(pl.multiple_of(start, 8), half), :]
            second = held[r, pl.ds(pl.multiple_of(start + half, 8), half), :]
            if r == 0:
                firsts[0][s * half : (s + 1) * half, :] = first
            else:
                coded, code = encode(first)
                firsts[r][s * half : (s + 1) * half, :] = coded
                first_codes.append(code)
            if s == 0:
                seconds[0][r * half : (r + 1) * half, :] = second
            else:
                coded, code = encode(second)
                seconds[s][r * half : (r + 1) * half, :] = coded
                second_codes[s].append(code)
        if r > 0:
            firsts[r][side * half :, :] = meta_rows(first_codes)
    for s in range(1, side):
        seconds[s][side * half :, :] = meta_rows(second_codes[s])


def product(place, up_weights, factor_left, factor_right, routed):
    experts, width, hidden = up_weights.shape
    rank = factor_left.shape[2]
    groups, _, capacity, _ = routed.shape
    rows = groups * capacity
    own = hidden // SIDE // 2
    parts = [(own, f32)] + [(own + 16, i16)] * (SIDE - 1)
    return pl.pallas_call(
        product_kernel,
        grid=(experts,),
        in_specs=[
            pl.BlockSpec(memory_space=pltpu.SMEM),
            pl.BlockSpec((1, width, hidden), lambda j: (j, 0, 0)),
            pl.BlockSpec((1, width, rank), lambda j: (j, 0, 0)),
            pl.BlockSpec((1, rank, hidden), lambda j: (j, 0, 0)),
            pl.BlockSpec((groups, 1, capacity, width), lambda j: (0, j, 0, 0)),
        ],
        out_specs=[pl.BlockSpec((height, rows), lambda j: (0, j)) for height, _ in parts * 2],
        out_shape=[jax.ShapeDtypeStruct((height, experts * rows), kind) for height, kind in parts * 2],
        scratch_shapes=[pltpu.VMEM((SIDE, hidden // SIDE, rows), f32)],
        compiler_params=params("arbitrary"),
        cost_estimate=pl.CostEstimate(
            flops=4 * experts * rows * width * hidden,
            bytes_accessed=4 * (up_weights.size + experts * rows * hidden),
            transcendentals=0,
        ),
        name="routed_product",
    )(place, up_weights, factor_left, factor_right, routed)


def base_product_kernel(place_ref, coded_ref, *refs):
    side = SIDE
    rows, outs, held = refs[:side], refs[side : 2 * side], refs[-1]
    groups, _, height, width = coded_ref.shape
    columns = held.shape[0] // side
    contract = (((0,), (1,)), ((), ()))
    value = None
    for r in range(side):
        part = decode_rows(coded_ref[:, r].reshape(groups * height, width))
        for term in split(part):
            added = lax.dot_general(term, rows[r][...], contract, preferred_element_type=f32)
            value = added if value is None else value + added
    held[...] = value
    for s in range(side):
        start = pl.multiple_of(lax.rem(place_ref[1] + s, side) * columns, 8)
        piece = held[pl.ds(start, columns), :]
        if s == 0:
            outs[0][...] = piece
        else:
            coded, code = encode(piece)
            outs[s][:columns, :] = coded
            outs[s][columns:, :] = meta_rows([code])


def base_product(place, coded, rows):
    groups, side, height, width = coded.shape
    tokens = rows[0].shape[0]
    block = width - META
    columns = block // side
    vmem = pl.BlockSpec(memory_space=pltpu.VMEM)
    return pl.pallas_call(
        base_product_kernel,
        in_specs=[pl.BlockSpec(memory_space=pltpu.SMEM)] + [vmem] * (side + 1),
        out_shape=[jax.ShapeDtypeStruct((columns, tokens), f32)]
        + [jax.ShapeDtypeStruct((columns + 16, tokens), i16)] * (side - 1),
        scratch_shapes=[pltpu.VMEM((block, tokens), f32)],
        compiler_params=params(),
        cost_estimate=pl.CostEstimate(
            flops=4 * groups * side * height * tokens * block,
            bytes_accessed=4 * groups * side * height * block,
            transcendentals=0,
        ),
        name="base_product",
    )(place, coded, *rows)


def fold_kernel(*refs):
    side = SIDE
    for which in range(2):
        own, others = refs[which * side], refs[which * side + 1 : (which + 1) * side]
        outs = refs[(2 + which) * side : (3 + which) * side]
        half = own.shape[0] // side
        for s in range(side):
            piece = slice(s * half, (s + 1) * half)
            value = own[piece, :]
            for other in others:
                code = from_i16(other[side * half :, :])[s : s + 1]
                value = value + from_i16(other[piece, :]) * down_scale(code)
            if s == 0:
                outs[0][...] = value
            else:
                coded, code = encode(value)
                outs[s][:half, :] = coded
                outs[s][half:, :] = meta_rows([code])


def fold(firsts, seconds):
    own, total = firsts[0].shape
    half = own // SIDE
    block = 512
    heights = [own] + [own + 16] * (SIDE - 1)
    parts = [(half, f32)] + [(half + 16, i16)] * (SIDE - 1)
    outs = pl.pallas_call(
        fold_kernel,
        grid=(total // block,),
        in_specs=[pl.BlockSpec((height, block), lambda j: (0, j)) for height in heights * 2],
        out_specs=[pl.BlockSpec((height, block), lambda j: (0, j)) for height, _ in parts * 2],
        out_shape=[jax.ShapeDtypeStruct((height, total), kind) for height, kind in parts * 2],
        compiler_params=params("arbitrary"),
        name="fold_sums",
    )(*firsts, *seconds)
    return outs[:SIDE], outs[SIDE:]


def pack_kernel(groups, experts, capacity, *refs):
    side = SIDE
    out_ref = refs[-1]
    halves = []
    for which in range(2):
        own, others = refs[which * side], refs[which * side + 1 : (which + 1) * side]
        half = own.shape[0]
        value = own[...]
        for other in others:
            code = from_i16(other[half:, :])[0:1]
            value = value + from_i16(other[:half, :]) * down_scale(code)
        halves.append(value)
    values = jnp.concatenate(halves, axis=0)
    columns = values.shape[0]
    span = groups * capacity
    for g in range(groups):
        value = jnp.concatenate(
            [values[:, j * span + g * capacity : j * span + (g + 1) * capacity] for j in range(experts)],
            axis=1,
        )
        coded, code = encode(value)
        out_ref[g, :columns, :] = coded
        out_ref[g, columns:, :] = meta_rows([code])


def pack(firsts, seconds, groups, experts, capacity):
    columns = 2 * firsts[0].shape[0]
    return pl.pallas_call(
        lambda *refs: pack_kernel(groups, experts, capacity, *refs),
        out_shape=jax.ShapeDtypeStruct((groups, columns + 16, experts * capacity), i16),
        compiler_params=params(),
        name="pack_result",
    )(*firsts, *seconds)


def step_to(dx, dy):
    side = SIDE
    return [
        (x * side + y, (x + dx) % side * side + (y + dy) % side)
        for x in range(side)
        for y in range(side)
    ]


def exchange(parts, along_x, sign=1):
    return [parts[0]] + [
        lax.ppermute(parts[r], "width", step_to(sign * r, 0) if along_x else step_to(0, sign * r))
        for r in range(1, SIDE)
    ]


def unpack_kernel(coded_ref, target_ref, *rest):
    own, others, out_ref = rest[0], rest[1:SIDE], rest[SIDE]
    groups, height, slots = coded_ref.shape
    columns, tokens = out_ref.shape
    target = target_ref[...]
    value = jnp.zeros((2 * columns, tokens), f32)
    for g in range(groups):
        part = from_i16(coded_ref[g])
        terms = split(part[:columns] * down_scale(part[columns : columns + 1]))
        place = lax.broadcasted_iota(i32, (slots, tokens), 0) + g * slots
        chosen = (place == target).astype(f32).astype(bf16)
        value = value + jnp.dot(jnp.concatenate(terms, axis=0), chosen, preferred_element_type=f32)
    base = own[...]
    for other in others:
        base = base + from_i16(other[:columns, :]) * down_scale(from_i16(other[columns:, :])[0:1])
    out_ref[...] = value[:columns] + value[columns:] - base


def unpack(coded, target, base_parts):
    groups, height, slots = coded.shape
    return pl.pallas_call(
        unpack_kernel,
        out_shape=jax.ShapeDtypeStruct((height - 16, target.shape[1]), f32),
        compiler_params=params(),
        name="unpack_result",
    )(coded, target, *base_parts)


def local(up_weights, fisher, factor_left, factor_right, calib_rows, routes):
    exp_local, width_rows, hidden = up_weights.shape
    groups = lax.axis_size("expert")
    expert_total = exp_local * groups
    capacity = 2 * calib_rows.shape[0] // expert_total

    index = lax.axis_index("width")
    place = jnp.stack([index // SIDE, index % SIDE]).astype(i32)

    rows_along_x = exchange([calib_rows] * SIDE, True)
    target, outgoing = route(routes, calib_rows, expert_total, capacity)
    incoming = lax.all_to_all(
        outgoing.reshape(groups, exp_local * capacity, width_rows), "expert", 0, 0, tiled=True
    )
    sums = exchange(weighted(place, up_weights, fisher), True)
    incoming, sums = lax.optimization_barrier((incoming, sums))
    parts = product(
        place,
        up_weights,
        factor_left,
        factor_right,
        incoming.reshape(groups, exp_local, capacity, width_rows),
    )
    parts, sums, rows_along_x = lax.optimization_barrier((parts, sums, rows_along_x))
    height, span = width_rows // groups, hidden // SIDE + META
    sums = jnp.stack([part.reshape(groups, height, span) for part in sums], axis=1)
    sums = lax.all_to_all(
        sums.reshape(groups, SIDE * height, span), "expert", 0, 0, tiled=True
    )
    firsts, seconds = exchange(parts[:SIDE], True), exchange(parts[SIDE:], False)
    coded_base = base_slice(sums)
    coded_base, firsts[1] = lax.optimization_barrier((coded_base, firsts[1]))
    coded_base = lax.all_gather(coded_base, "expert", tiled=True)
    coded_base = coded_base.reshape(groups, SIDE, height, span)
    coded_base, firsts, seconds = lax.optimization_barrier((coded_base, firsts, seconds))
    firsts, seconds = fold(firsts, seconds)
    base_parts = base_product(place, coded_base, rows_along_x)
    firsts, seconds = exchange(firsts, False), exchange(seconds, True)
    firsts[0], base_parts = lax.optimization_barrier((firsts[0], base_parts))
    base_parts = exchange(base_parts, False)
    values = pack(firsts, seconds, groups, exp_local, capacity)
    returned = lax.all_to_all(values, "expert", 0, 0, tiled=True)
    chunks = [coded_base[:, r].reshape(width_rows, span) for r in range(SIDE)]
    shared_base = shared(place, exchange(chunks, True, -1))
    return shared_base, unpack(returned, target, base_parts).T


def solution(mesh):
    placed = (
        P("expert", "width", None),
        P("expert", "width"),
        P("expert", "width", None),
        P("expert", None, None),
        P("expert", "width"),
        P("expert", None),
    )
    return jax.shard_map(
        local,
        mesh=mesh,
        in_specs=placed,
        out_specs=(P("width", None), P("expert", "width")),
        check_vma=False,
    )
```

```python
import jax
import jax.numpy as jnp
from jax import lax
from jax.experimental import pallas as pl
from jax.experimental.pallas import tpu as pltpu
from jax.sharding import PartitionSpec as P

f32, bf16, i16, i32 = jnp.float32, jnp.bfloat16, jnp.int16, jnp.int32
VMEM_LIMIT = 48 * 1024 * 1024
TOP = 32000.0
STEPS = 64.0
META = 128
SIDE = 4


def scale_code(biggest):
    return jnp.ceil(jnp.log2(jnp.maximum(biggest, 2.0**-100)) * STEPS) + 1.0


def up_scale(code):
    return jnp.exp2(code * (-1.0 / STEPS)) * TOP


def down_scale(code):
    return jnp.exp2(code * (1.0 / STEPS)) * (1.0 / TOP)


def to_i16(x):
    return jnp.round(x).astype(i32).astype(i16)


def from_i16(x):
    return x.astype(i32).astype(f32)


def params(*semantics):
    return pltpu.CompilerParams(dimension_semantics=semantics or None, vmem_limit_bytes=VMEM_LIMIT)


def weighted_kernel(place_ref, up_ref, fisher_ref, *outs):
    experts, rows, hidden = up_ref.shape
    block = hidden // SIDE
    total = fisher_ref[:, 0:1]
    for j in range(1, experts):
        total = total + fisher_ref[:, j : j + 1]
    fixed = jnp.round(total * 2.0**20).astype(i32)
    lane = lax.broadcasted_iota(i32, (rows, META), 1)
    fixed = jnp.where(lane < 64, fixed >> 15, fixed & 32767)
    for r in range(SIDE):
        part = pl.ds(pl.multiple_of(lax.rem(place_ref[0] + r, SIDE) * block, META), block)
        value = fisher_ref[:, 0:1] * up_ref[0, :, part]
        for j in range(1, experts):
            value = value + fisher_ref[:, j : j + 1] * up_ref[j, :, part]
        code = scale_code(jnp.max(jnp.abs(value), axis=1, keepdims=True))
        outs[r][:, :block] = to_i16(value * up_scale(code))
        outs[r][:, block:] = jnp.where(lane < 32, code.astype(i32), fixed).astype(i16)


def weighted(place, up_weights, fisher):
    experts, rows, hidden = up_weights.shape
    block = 64
    width = hidden // SIDE + META
    return pl.pallas_call(
        weighted_kernel,
        grid=(rows // block,),
        in_specs=[
            pl.BlockSpec(memory_space=pltpu.SMEM),
            pl.BlockSpec((experts, block, hidden), lambda i: (0, i, 0)),
            pl.BlockSpec((block, experts), lambda i: (i, 0)),
        ],
        out_specs=[pl.BlockSpec((block, width), lambda i: (i, 0))] * SIDE,
        out_shape=[jax.ShapeDtypeStruct((rows, width), i16)] * SIDE,
        compiler_params=params("arbitrary"),
        cost_estimate=pl.CostEstimate(
            flops=2 * up_weights.size, bytes_accessed=4 * up_weights.size, transcendentals=0
        ),
        name="weighted_sum",
    )(place, up_weights, fisher.T)


def base_kernel(parts_ref, out_ref):
    groups, rows, width = parts_ref.shape
    hidden = width - META
    value = jnp.zeros((rows, hidden), f32)
    total = jnp.zeros((rows, 1), f32)
    for g in range(groups):
        part = from_i16(parts_ref[g])
        value = value + part[:, :hidden] * down_scale(part[:, hidden : hidden + 1])
        total = total + (part[:, hidden + 32 : hidden + 33] * 32768.0 + part[:, hidden + 64 : hidden + 65])
    base = value * (2.0**20 / total)
    code = scale_code(jnp.max(jnp.abs(base), axis=1, keepdims=True))
    out_ref[:, :hidden] = to_i16(base * up_scale(code))
    out_ref[:, hidden:] = jnp.broadcast_to(code.astype(i32), (rows, META)).astype(i16)


def base_slice(parts):
    groups, rows, width = parts.shape
    return pl.pallas_call(
        base_kernel,
        out_shape=jax.ShapeDtypeStruct((rows, width), i16),
        compiler_params=params(),
        name="base_slice",
    )(parts)


def decode_rows(coded):
    block = coded.shape[1] - META
    return from_i16(coded[:, :block]) * down_scale(from_i16(coded[:, block:])[:, 0:1])


def shared_kernel(place_ref, *refs):
    out_ref = refs[-1]
    block = out_ref.shape[1] // SIDE
    for r in range(SIDE):
        start = pl.multiple_of(lax.rem(place_ref[0] + r, SIDE) * block, META)
        out_ref[:, pl.ds(start, block)] = decode_rows(refs[r][...])


def shared(place, codeds):
    rows, width = codeds[0].shape
    vmem = pl.BlockSpec(memory_space=pltpu.VMEM)
    return pl.pallas_call(
        shared_kernel,
        in_specs=[pl.BlockSpec(memory_space=pltpu.SMEM)] + [vmem] * SIDE,
        out_shape=jax.ShapeDtypeStruct((rows, (width - META) * SIDE), f32),
        compiler_params=params(),
        name="shared_base",
    )(place, *codeds)


def route_kernel(experts, capacity, routes_ref, rows_ref, target_ref, out_ref):
    tokens = rows_ref.shape[0]
    block = out_ref.shape[0]
    step = pl.program_id(0)

    @pl.when(step == 0)
    def _():
        routes = routes_ref[...]
        hit = lax.broadcasted_iota(i32, (experts, tokens), 0) == routes
        one_hot = hit.astype(f32).astype(bf16)
        before = lax.broadcasted_iota(i32, (tokens, tokens), 0) < lax.broadcasted_iota(
            i32, (tokens, tokens), 1
        )
        earlier = jnp.dot(one_hot, before.astype(f32).astype(bf16), preferred_element_type=f32)
        slot = jnp.sum(jnp.where(hit, earlier, 0.0), axis=0, keepdims=True)
        target_ref[...] = routes * capacity + slot.astype(i32)

    place = lax.broadcasted_iota(i32, (block, tokens), 0) + step * block
    chosen = (place == target_ref[...]).astype(f32).astype(bf16)
    out_ref[...] = jnp.dot(chosen, rows_ref[...], preferred_element_type=f32).astype(bf16)


def route(routes, calib_rows, experts, capacity):
    tokens, width = calib_rows.shape
    slots = experts * capacity
    block = 256
    return pl.pallas_call(
        lambda *refs: route_kernel(experts, capacity, *refs),
        grid=(slots // block,),
        in_specs=[
            pl.BlockSpec((1, tokens), lambda i: (0, 0)),
            pl.BlockSpec((tokens, width), lambda i: (0, 0)),
        ],
        out_specs=[
            pl.BlockSpec((1, tokens), lambda i: (0, 0)),
            pl.BlockSpec((block, width), lambda i: (i, 0)),
        ],
        out_shape=[
            jax.ShapeDtypeStruct((1, tokens), i32),
            jax.ShapeDtypeStruct((slots, width), bf16),
        ],
        compiler_params=params("arbitrary"),
        cost_estimate=pl.CostEstimate(
            flops=2 * slots * tokens * width, bytes_accessed=4 * slots * width, transcendentals=0
        ),
        name="route_rows",
    )(routes.reshape(1, tokens), calib_rows)


def meta_rows(codes):
    lanes = codes[0].shape[1]
    row = lax.broadcasted_iota(i32, (16, lanes), 0)
    meta = jnp.zeros((16, lanes), i32)
    for position, code in enumerate(codes):
        meta = jnp.where(row == position, code.astype(i32), meta)
    return meta.astype(i16)


def split(value):
    high = value.astype(bf16)
    return high, (value - high.astype(f32)).astype(bf16)


def encode(value):
    code = scale_code(jnp.max(jnp.abs(value), axis=0, keepdims=True))
    return to_i16(value * up_scale(code)), code


def product_kernel(place_ref, up_ref, left_ref, right_ref, rows_ref, *rest):
    side = SIDE
    firsts, seconds, held = rest[:side], rest[side : 2 * side], rest[2 * side]
    _, width, hidden = up_ref.shape
    block = hidden // side
    columns = block // side
    half = columns // 2

    groups, _, capacity, _ = rows_ref.shape
    rows = rows_ref[:, 0].reshape(groups * capacity, width)
    contract = (((0,), (1,)), ((), ()))
    second_codes = [[] for s in range(side)]
    left_high, left_low = split(left_ref[0])
    left_all = jnp.concatenate([left_high, left_low], axis=1)
    for r in range(side):
        part = pl.ds(pl.multiple_of(lax.rem(place_ref[0] + r, side) * block, block), block)
        right_high, right_low = split(right_ref[0, :, part])
        low_rank = jnp.dot(
            left_all, jnp.concatenate([right_high] * 2, axis=0), preferred_element_type=f32
        ) + jnp.dot(left_high, right_low, preferred_element_type=f32)
        high, low = split(up_ref[0, :, part] - low_rank)
        held[r] = lax.dot_general(high, rows, contract, preferred_element_type=f32) + lax.dot_general(
            low, rows, contract, preferred_element_type=f32
        )
        first_codes = []
        for s in range(side):
            start = lax.rem(place_ref[1] + s, side) * columns
            first = held[r, pl.ds(pl.multiple_of(start, 8), half), :]
            second = held[r, pl.ds(pl.multiple_of(start + half, 8), half), :]
            if r == 0:
                firsts[0][s * half : (s + 1) * half, :] = first
            else:
                coded, code = encode(first)
                firsts[r][s * half : (s + 1) * half, :] = coded
                first_codes.append(code)
            if s == 0:
                seconds[0][r * half : (r + 1) * half, :] = second
            else:
                coded, code = encode(second)
                seconds[s][r * half : (r + 1) * half, :] = coded
                second_codes[s].append(code)
        if r > 0:
            firsts[r][side * half :, :] = meta_rows(first_codes)
    for s in range(1, side):
        seconds[s][side * half :, :] = meta_rows(second_codes[s])


def product(place, up_weights, factor_left, factor_right, routed):
    experts, width, hidden = up_weights.shape
    rank = factor_left.shape[2]
    groups, _, capacity, _ = routed.shape
    rows = groups * capacity
    own = hidden // SIDE // 2
    parts = [(own, f32)] + [(own + 16, i16)] * (SIDE - 1)
    return pl.pallas_call(
        product_kernel,
        grid=(experts,),
        in_specs=[
            pl.BlockSpec(memory_space=pltpu.SMEM),
            pl.BlockSpec((1, width, hidden), lambda j: (j, 0, 0)),
            pl.BlockSpec((1, width, rank), lambda j: (j, 0, 0)),
            pl.BlockSpec((1, rank, hidden), lambda j: (j, 0, 0)),
            pl.BlockSpec((groups, 1, capacity, width), lambda j: (0, j, 0, 0)),
        ],
        out_specs=[pl.BlockSpec((height, rows), lambda j: (0, j)) for height, _ in parts * 2],
        out_shape=[jax.ShapeDtypeStruct((height, experts * rows), kind) for height, kind in parts * 2],
        scratch_shapes=[pltpu.VMEM((SIDE, hidden // SIDE, rows), f32)],
        compiler_params=params("arbitrary"),
        cost_estimate=pl.CostEstimate(
            flops=4 * experts * rows * width * hidden,
            bytes_accessed=4 * (up_weights.size + experts * rows * hidden),
            transcendentals=0,
        ),
        name="routed_product",
    )(place, up_weights, factor_left, factor_right, routed)


def base_product_kernel(place_ref, coded_ref, *refs):
    side = SIDE
    rows, outs, held = refs[:side], refs[side : 2 * side], refs[-1]
    groups, _, height, width = coded_ref.shape
    columns = held.shape[0] // side
    contract = (((0,), (1,)), ((), ()))
    value = None
    for r in range(side):
        part = decode_rows(coded_ref[:, r].reshape(groups * height, width))
        for term in split(part):
            added = lax.dot_general(term, rows[r][...], contract, preferred_element_type=f32)
            value = added if value is None else value + added
    held[...] = value
    for s in range(side):
        start = pl.multiple_of(lax.rem(place_ref[1] + s, side) * columns, 8)
        piece = held[pl.ds(start, columns), :]
        if s == 0:
            outs[0][...] = piece
        else:
            coded, code = encode(piece)
            outs[s][:columns, :] = coded
            outs[s][columns:, :] = meta_rows([code])


def base_product(place, coded, rows):
    groups, side, height, width = coded.shape
    tokens = rows[0].shape[0]
    block = width - META
    columns = block // side
    vmem = pl.BlockSpec(memory_space=pltpu.VMEM)
    return pl.pallas_call(
        base_product_kernel,
        in_specs=[pl.BlockSpec(memory_space=pltpu.SMEM)] + [vmem] * (side + 1),
        out_shape=[jax.ShapeDtypeStruct((columns, tokens), f32)]
        + [jax.ShapeDtypeStruct((columns + 16, tokens), i16)] * (side - 1),
        scratch_shapes=[pltpu.VMEM((block, tokens), f32)],
        compiler_params=params(),
        cost_estimate=pl.CostEstimate(
            flops=4 * groups * side * height * tokens * block,
            bytes_accessed=4 * groups * side * height * block,
            transcendentals=0,
        ),
        name="base_product",
    )(place, coded, *rows)


def fold_kernel(*refs):
    side = SIDE
    for which in range(2):
        own, others = refs[which * side], refs[which * side + 1 : (which + 1) * side]
        outs = refs[(2 + which) * side : (3 + which) * side]
        half = own.shape[0] // side
        for s in range(side):
            piece = slice(s * half, (s + 1) * half)
            value = own[piece, :]
            for other in others:
                code = from_i16(other[side * half :, :])[s : s + 1]
                value = value + from_i16(other[piece, :]) * down_scale(code)
            if s == 0:
                outs[0][...] = value
            else:
                coded, code = encode(value)
                outs[s][:half, :] = coded
                outs[s][half:, :] = meta_rows([code])


def fold(firsts, seconds):
    own, total = firsts[0].shape
    half = own // SIDE
    block = 512
    heights = [own] + [own + 16] * (SIDE - 1)
    parts = [(half, f32)] + [(half + 16, i16)] * (SIDE - 1)
    outs = pl.pallas_call(
        fold_kernel,
        grid=(total // block,),
        in_specs=[pl.BlockSpec((height, block), lambda j: (0, j)) for height in heights * 2],
        out_specs=[pl.BlockSpec((height, block), lambda j: (0, j)) for height, _ in parts * 2],
        out_shape=[jax.ShapeDtypeStruct((height, total), kind) for height, kind in parts * 2],
        compiler_params=params("arbitrary"),
        name="fold_sums",
    )(*firsts, *seconds)
    return outs[:SIDE], outs[SIDE:]


def pack_kernel(groups, experts, capacity, *refs):
    side = SIDE
    out_ref = refs[-1]
    halves = []
    for which in range(2):
        own, others = refs[which * side], refs[which * side + 1 : (which + 1) * side]
        half = own.shape[0]
        value = own[...]
        for other in others:
            code = from_i16(other[half:, :])[0:1]
            value = value + from_i16(other[:half, :]) * down_scale(code)
        halves.append(value)
    values = jnp.concatenate(halves, axis=0)
    columns = values.shape[0]
    span = groups * capacity
    for g in range(groups):
        value = jnp.concatenate(
            [values[:, j * span + g * capacity : j * span + (g + 1) * capacity] for j in range(experts)],
            axis=1,
        )
        coded, code = encode(value)
        out_ref[g, :columns, :] = coded
        out_ref[g, columns:, :] = meta_rows([code])


def pack(firsts, seconds, groups, experts, capacity):
    columns = 2 * firsts[0].shape[0]
    return pl.pallas_call(
        lambda *refs: pack_kernel(groups, experts, capacity, *refs),
        out_shape=jax.ShapeDtypeStruct((groups, columns + 16, experts * capacity), i16),
        compiler_params=params(),
        name="pack_result",
    )(*firsts, *seconds)


def step_to(dx, dy):
    side = SIDE
    return [
        (x * side + y, (x + dx) % side * side + (y + dy) % side)
        for x in range(side)
        for y in range(side)
    ]


def exchange(parts, along_x, sign=1):
    return [parts[0]] + [
        lax.ppermute(parts[r], "width", step_to(sign * r, 0) if along_x else step_to(0, sign * r))
        for r in range(1, SIDE)
    ]


def unpack_kernel(coded_ref, target_ref, *rest):
    own, others, out_ref = rest[0], rest[1:SIDE], rest[SIDE]
    groups, height, slots = coded_ref.shape
    columns, tokens = out_ref.shape
    target = target_ref[...]
    value = jnp.zeros((2 * columns, tokens), f32)
    for g in range(groups):
        part = from_i16(coded_ref[g])
        terms = split(part[:columns] * down_scale(part[columns : columns + 1]))
        place = lax.broadcasted_iota(i32, (slots, tokens), 0) + g * slots
        chosen = (place == target).astype(f32).astype(bf16)
        value = value + jnp.dot(jnp.concatenate(terms, axis=0), chosen, preferred_element_type=f32)
    base = own[...]
    for other in others:
        base = base + from_i16(other[:columns, :]) * down_scale(from_i16(other[columns:, :])[0:1])
    out_ref[...] = value[:columns] + value[columns:] - base


def unpack(coded, target, base_parts):
    groups, height, slots = coded.shape
    return pl.pallas_call(
        unpack_kernel,
        out_shape=jax.ShapeDtypeStruct((height - 16, target.shape[1]), f32),
        compiler_params=params(),
        name="unpack_result",
    )(coded, target, *base_parts)


def local(up_weights, fisher, factor_left, factor_right, calib_rows, routes):
    exp_local, width_rows, hidden = up_weights.shape
    groups = lax.axis_size("expert")
    expert_total = exp_local * groups
    capacity = 2 * calib_rows.shape[0] // expert_total

    index = lax.axis_index("width")
    place = jnp.stack([index // SIDE, index % SIDE]).astype(i32)

    rows_along_x = exchange([calib_rows] * SIDE, True)
    target, outgoing = route(routes, calib_rows, expert_total, capacity)
    incoming = lax.all_to_all(
        outgoing.reshape(groups, exp_local * capacity, width_rows), "expert", 0, 0, tiled=True
    )
    sums = exchange(weighted(place, up_weights, fisher), True)
    incoming, sums = lax.optimization_barrier((incoming, sums))
    near = [rows_along_x[r] for r in (1, SIDE - 1)]
    sums, near = lax.optimization_barrier((sums, near))
    rows_along_x[1], rows_along_x[SIDE - 1] = near
    parts = product(
        place,
        up_weights,
        factor_left,
        factor_right,
        incoming.reshape(groups, exp_local, capacity, width_rows),
    )
    parts, rows_along_x[2] = lax.optimization_barrier((parts, rows_along_x[2]))
    height, span = width_rows // groups, hidden // SIDE + META
    sums = jnp.stack([part.reshape(groups, height, span) for part in sums], axis=1)
    sums = lax.all_to_all(
        sums.reshape(groups, SIDE * height, span), "expert", 0, 0, tiled=True
    )
    firsts, seconds = exchange(parts[:SIDE], True), exchange(parts[SIDE:], False)
    coded_base = base_slice(sums)
    coded_base, firsts[1] = lax.optimization_barrier((coded_base, firsts[1]))
    coded_base = lax.all_gather(coded_base, "expert", tiled=True)
    coded_base = coded_base.reshape(groups, SIDE, height, span)
    coded_base, firsts, seconds = lax.optimization_barrier((coded_base, firsts, seconds))
    firsts, seconds = fold(firsts, seconds)
    base_parts = exchange(base_product(place, coded_base, rows_along_x), False)
    firsts, seconds = exchange(firsts, False), exchange(seconds, True)
    values = pack(firsts, seconds, groups, exp_local, capacity)
    returned = lax.all_to_all(values, "expert", 0, 0, tiled=True)
    chunks = [coded_base[:, r].reshape(width_rows, span) for r in range(SIDE)]
    shared_base = shared(place, exchange(chunks, True, -1))
    return shared_base, unpack(returned, target, base_parts).T


def solution(mesh):
    placed = (
        P("expert", "width", None),
        P("expert", "width"),
        P("expert", "width", None),
        P("expert", None, None),
        P("expert", "width"),
        P("expert", None),
    )
    return jax.shard_map(
        local,
        mesh=mesh,
        in_specs=placed,
        out_specs=(P("width", None), P("expert", "width")),
        check_vma=False,
    )
```

```python
import jax
import jax.numpy as jnp
from jax import lax
from jax.experimental import pallas as pl
from jax.experimental.pallas import tpu as pltpu
from jax.sharding import PartitionSpec as P

f32, bf16, i16, i32 = jnp.float32, jnp.bfloat16, jnp.int16, jnp.int32
VMEM_LIMIT = 48 * 1024 * 1024
TOP = 32000.0
STEPS = 64.0
META = 128
SIDE = 4


def scale_code(biggest):
    return jnp.ceil(jnp.log2(jnp.maximum(biggest, 2.0**-100)) * STEPS) + 1.0


def up_scale(code):
    return jnp.exp2(code * (-1.0 / STEPS)) * TOP


def down_scale(code):
    return jnp.exp2(code * (1.0 / STEPS)) * (1.0 / TOP)


def to_i16(x):
    return jnp.round(x).astype(i32).astype(i16)


def from_i16(x):
    return x.astype(i32).astype(f32)


def params(*semantics):
    return pltpu.CompilerParams(dimension_semantics=semantics or None, vmem_limit_bytes=VMEM_LIMIT)


def weighted_kernel(place_ref, up_ref, fisher_ref, *outs):
    experts, rows, hidden = up_ref.shape
    block = hidden // SIDE
    total = fisher_ref[:, 0:1]
    for j in range(1, experts):
        total = total + fisher_ref[:, j : j + 1]
    fixed = jnp.round(total * 2.0**20).astype(i32)
    lane = lax.broadcasted_iota(i32, (rows, META), 1)
    fixed = jnp.where(lane < 64, fixed >> 15, fixed & 32767)
    for r in range(SIDE):
        part = pl.ds(pl.multiple_of(lax.rem(place_ref[0] + r, SIDE) * block, META), block)
        value = fisher_ref[:, 0:1] * up_ref[0, :, part]
        for j in range(1, experts):
            value = value + fisher_ref[:, j : j + 1] * up_ref[j, :, part]
        code = scale_code(jnp.max(jnp.abs(value), axis=1, keepdims=True))
        outs[r][:, :block] = to_i16(value * up_scale(code))
        outs[r][:, block:] = jnp.where(lane < 32, code.astype(i32), fixed).astype(i16)


def weighted(place, up_weights, fisher):
    experts, rows, hidden = up_weights.shape
    block = 64
    width = hidden // SIDE + META
    return pl.pallas_call(
        weighted_kernel,
        grid=(rows // block,),
        in_specs=[
            pl.BlockSpec(memory_space=pltpu.SMEM),
            pl.BlockSpec((experts, block, hidden), lambda i: (0, i, 0)),
            pl.BlockSpec((block, experts), lambda i: (i, 0)),
        ],
        out_specs=[pl.BlockSpec((block, width), lambda i: (i, 0))] * SIDE,
        out_shape=[jax.ShapeDtypeStruct((rows, width), i16)] * SIDE,
        compiler_params=params("arbitrary"),
        cost_estimate=pl.CostEstimate(
            flops=2 * up_weights.size, bytes_accessed=4 * up_weights.size, transcendentals=0
        ),
        name="weighted_sum",
    )(place, up_weights, fisher.T)


def base_kernel(parts_ref, out_ref):
    groups, rows, width = parts_ref.shape
    hidden = width - META
    value = jnp.zeros((rows, hidden), f32)
    total = jnp.zeros((rows, 1), f32)
    for g in range(groups):
        part = from_i16(parts_ref[g])
        value = value + part[:, :hidden] * down_scale(part[:, hidden : hidden + 1])
        total = total + (part[:, hidden + 32 : hidden + 33] * 32768.0 + part[:, hidden + 64 : hidden + 65])
    base = value * (2.0**20 / total)
    code = scale_code(jnp.max(jnp.abs(base), axis=1, keepdims=True))
    out_ref[:, :hidden] = to_i16(base * up_scale(code))
    out_ref[:, hidden:] = jnp.broadcast_to(code.astype(i32), (rows, META)).astype(i16)


def base_slice(parts):
    groups, rows, width = parts.shape
    return pl.pallas_call(
        base_kernel,
        out_shape=jax.ShapeDtypeStruct((rows, width), i16),
        compiler_params=params(),
        name="base_slice",
    )(parts)


def decode_rows(coded):
    block = coded.shape[1] - META
    return from_i16(coded[:, :block]) * down_scale(from_i16(coded[:, block:])[:, 0:1])


def shared_kernel(place_ref, *refs):
    out_ref = refs[-1]
    block = out_ref.shape[1] // SIDE
    for r in range(SIDE):
        start = pl.multiple_of(lax.rem(place_ref[0] + r, SIDE) * block, META)
        out_ref[:, pl.ds(start, block)] = decode_rows(refs[r][...])


def shared(place, codeds):
    rows, width = codeds[0].shape
    vmem = pl.BlockSpec(memory_space=pltpu.VMEM)
    return pl.pallas_call(
        shared_kernel,
        in_specs=[pl.BlockSpec(memory_space=pltpu.SMEM)] + [vmem] * SIDE,
        out_shape=jax.ShapeDtypeStruct((rows, (width - META) * SIDE), f32),
        compiler_params=params(),
        name="shared_base",
    )(place, *codeds)


def route_kernel(experts, capacity, routes_ref, rows_ref, target_ref, out_ref):
    tokens = rows_ref.shape[0]
    block = out_ref.shape[0]
    step = pl.program_id(0)

    @pl.when(step == 0)
    def _():
        routes = routes_ref[...]
        hit = lax.broadcasted_iota(i32, (experts, tokens), 0) == routes
        one_hot = hit.astype(f32).astype(bf16)
        before = lax.broadcasted_iota(i32, (tokens, tokens), 0) < lax.broadcasted_iota(
            i32, (tokens, tokens), 1
        )
        earlier = jnp.dot(one_hot, before.astype(f32).astype(bf16), preferred_element_type=f32)
        slot = jnp.sum(jnp.where(hit, earlier, 0.0), axis=0, keepdims=True)
        target_ref[...] = routes * capacity + slot.astype(i32)

    place = lax.broadcasted_iota(i32, (block, tokens), 0) + step * block
    chosen = (place == target_ref[...]).astype(f32).astype(bf16)
    out_ref[...] = jnp.dot(chosen, rows_ref[...], preferred_element_type=f32).astype(bf16)


def route(routes, calib_rows, experts, capacity):
    tokens, width = calib_rows.shape
    slots = experts * capacity
    block = 256
    return pl.pallas_call(
        lambda *refs: route_kernel(experts, capacity, *refs),
        grid=(slots // block,),
        in_specs=[
            pl.BlockSpec((1, tokens), lambda i: (0, 0)),
            pl.BlockSpec((tokens, width), lambda i: (0, 0)),
        ],
        out_specs=[
            pl.BlockSpec((1, tokens), lambda i: (0, 0)),
            pl.BlockSpec((block, width), lambda i: (i, 0)),
        ],
        out_shape=[
            jax.ShapeDtypeStruct((1, tokens), i32),
            jax.ShapeDtypeStruct((slots, width), bf16),
        ],
        compiler_params=params("arbitrary"),
        cost_estimate=pl.CostEstimate(
            flops=2 * slots * tokens * width, bytes_accessed=4 * slots * width, transcendentals=0
        ),
        name="route_rows",
    )(routes.reshape(1, tokens), calib_rows)


def meta_rows(codes):
    lanes = codes[0].shape[1]
    row = lax.broadcasted_iota(i32, (16, lanes), 0)
    meta = jnp.zeros((16, lanes), i32)
    for position, code in enumerate(codes):
        meta = jnp.where(row == position, code.astype(i32), meta)
    return meta.astype(i16)


def split(value):
    high = value.astype(bf16)
    return high, (value - high.astype(f32)).astype(bf16)


def encode(value):
    code = scale_code(jnp.max(jnp.abs(value), axis=0, keepdims=True))
    return to_i16(value * up_scale(code)), code


def product_kernel(place_ref, up_ref, left_ref, right_ref, rows_ref, *rest):
    side = SIDE
    firsts, seconds, held = rest[:side], rest[side : 2 * side], rest[2 * side]
    _, width, hidden = up_ref.shape
    block = hidden // side
    columns = block // side
    half = columns // 2

    groups, _, capacity, _ = rows_ref.shape
    rows = rows_ref[:, 0].reshape(groups * capacity, width)
    contract = (((0,), (1,)), ((), ()))
    second_codes = [[] for s in range(side)]
    left_high, left_low = split(left_ref[0])
    left_all = jnp.concatenate([left_high, left_low], axis=1)
    for r in range(side):
        part = pl.ds(pl.multiple_of(lax.rem(place_ref[0] + r, side) * block, block), block)
        right_high, right_low = split(right_ref[0, :, part])
        low_rank = jnp.dot(
            left_all, jnp.concatenate([right_high] * 2, axis=0), preferred_element_type=f32
        ) + jnp.dot(left_high, right_low, preferred_element_type=f32)
        high, low = split(up_ref[0, :, part] - low_rank)
        held[r] = lax.dot_general(high, rows, contract, preferred_element_type=f32) + lax.dot_general(
            low, rows, contract, preferred_element_type=f32
        )
        first_codes = []
        for s in range(side):
            start = lax.rem(place_ref[1] + s, side) * columns
            first = held[r, pl.ds(pl.multiple_of(start, 8), half), :]
            second = held[r, pl.ds(pl.multiple_of(start + half, 8), half), :]
            if r == 0:
                firsts[0][s * half : (s + 1) * half, :] = first
            else:
                coded, code = encode(first)
                firsts[r][s * half : (s + 1) * half, :] = coded
                first_codes.append(code)
            if s == 0:
                seconds[0][r * half : (r + 1) * half, :] = second
            else:
                coded, code = encode(second)
                seconds[s][r * half : (r + 1) * half, :] = coded
                second_codes[s].append(code)
        if r > 0:
            firsts[r][side * half :, :] = meta_rows(first_codes)
    for s in range(1, side):
        seconds[s][side * half :, :] = meta_rows(second_codes[s])


def product(place, up_weights, factor_left, factor_right, routed):
    experts, width, hidden = up_weights.shape
    rank = factor_left.shape[2]
    groups, _, capacity, _ = routed.shape
    rows = groups * capacity
    own = hidden // SIDE // 2
    parts = [(own, f32)] + [(own + 16, i16)] * (SIDE - 1)
    return pl.pallas_call(
        product_kernel,
        grid=(experts,),
        in_specs=[
            pl.BlockSpec(memory_space=pltpu.SMEM),
            pl.BlockSpec((1, width, hidden), lambda j: (j, 0, 0)),
            pl.BlockSpec((1, width, rank), lambda j: (j, 0, 0)),
            pl.BlockSpec((1, rank, hidden), lambda j: (j, 0, 0)),
            pl.BlockSpec((groups, 1, capacity, width), lambda j: (0, j, 0, 0)),
        ],
        out_specs=[pl.BlockSpec((height, rows), lambda j: (0, j)) for height, _ in parts * 2],
        out_shape=[jax.ShapeDtypeStruct((height, experts * rows), kind) for height, kind in parts * 2],
        scratch_shapes=[pltpu.VMEM((SIDE, hidden // SIDE, rows), f32)],
        compiler_params=params("arbitrary"),
        cost_estimate=pl.CostEstimate(
            flops=4 * experts * rows * width * hidden,
            bytes_accessed=4 * (up_weights.size + experts * rows * hidden),
            transcendentals=0,
        ),
        name="routed_product",
    )(place, up_weights, factor_left, factor_right, routed)


def base_product_kernel(place_ref, coded_ref, *refs):
    side = SIDE
    rows, outs, held = refs[:side], refs[side : 2 * side], refs[-1]
    groups, _, height, width = coded_ref.shape
    columns = held.shape[0] // side
    contract = (((0,), (1,)), ((), ()))
    value = None
    for r in range(side):
        part = decode_rows(coded_ref[:, r].reshape(groups * height, width))
        for term in split(part):
            added = lax.dot_general(term, rows[r][...], contract, preferred_element_type=f32)
            value = added if value is None else value + added
    held[...] = value
    for s in range(side):
        start = pl.multiple_of(lax.rem(place_ref[1] + s, side) * columns, 8)
        piece = held[pl.ds(start, columns), :]
        if s == 0:
            outs[0][...] = piece
        else:
            coded, code = encode(piece)
            outs[s][:columns, :] = coded
            outs[s][columns:, :] = meta_rows([code])


def base_product(place, coded, rows):
    groups, side, height, width = coded.shape
    tokens = rows[0].shape[0]
    block = width - META
    columns = block // side
    vmem = pl.BlockSpec(memory_space=pltpu.VMEM)
    return pl.pallas_call(
        base_product_kernel,
        in_specs=[pl.BlockSpec(memory_space=pltpu.SMEM)] + [vmem] * (side + 1),
        out_shape=[jax.ShapeDtypeStruct((columns, tokens), f32)]
        + [jax.ShapeDtypeStruct((columns + 16, tokens), i16)] * (side - 1),
        scratch_shapes=[pltpu.VMEM((block, tokens), f32)],
        compiler_params=params(),
        cost_estimate=pl.CostEstimate(
            flops=4 * groups * side * height * tokens * block,
            bytes_accessed=4 * groups * side * height * block,
            transcendentals=0,
        ),
        name="base_product",
    )(place, coded, *rows)


def merge_kernel(*refs):
    outs = refs[-4:]
    for which in range(4):
        coded, passed, out_ref = refs[2 * which], refs[2 * which + 1], outs[which]
        half = (coded.shape[0] - 16) // SIDE
        lanes = passed.shape[1]
        start = (which % 2) * lanes
        here, there = slice(start, start + lanes), slice(lanes - start, 2 * lanes - start)
        out_ref[:, there] = coded[:, there]
        own_codes, passed_codes = from_i16(coded[SIDE * half :, here]), from_i16(passed[SIDE * half :, :])
        codes = []
        for s in range(SIDE):
            piece = slice(s * half, (s + 1) * half)
            value = from_i16(coded[piece, here]) * down_scale(own_codes[s : s + 1])
            value = value + from_i16(passed[piece, :]) * down_scale(passed_codes[s : s + 1])
            summed, code = encode(value)
            out_ref[piece, here] = summed
            codes.append(code)
        out_ref[SIDE * half :, here] = meta_rows(codes)


def merge(first, second):
    operands = [*first, *second]
    shape = operands[0].shape
    return pl.pallas_call(
        merge_kernel,
        out_shape=[jax.ShapeDtypeStruct(shape, i16)] * 4,
        compiler_params=params(),
        name="merge_parts",
    )(*operands)


def fold_kernel(*refs):
    side, given = SIDE, 3
    for which in range(2):
        own, others = refs[which * given], refs[which * given + 1 : (which + 1) * given]
        outs = refs[2 * given + which * side : 2 * given + (which + 1) * side]
        half = own.shape[0] // side
        for s in range(side):
            piece = slice(s * half, (s + 1) * half)
            value = own[piece, :]
            for other in others:
                code = from_i16(other[side * half :, :])[s : s + 1]
                value = value + from_i16(other[piece, :]) * down_scale(code)
            if s == 0:
                outs[0][...] = value
            else:
                coded, code = encode(value)
                outs[s][:half, :] = coded
                outs[s][half:, :] = meta_rows([code])


def fold(firsts, seconds):
    own, total = firsts[0].shape
    half = own // SIDE
    block = 512
    heights = [own] + [own + 16] * 2
    parts = [(half, f32)] + [(half + 16, i16)] * (SIDE - 1)
    outs = pl.pallas_call(
        fold_kernel,
        grid=(total // block,),
        in_specs=[pl.BlockSpec((height, block), lambda j: (0, j)) for height in heights * 2],
        out_specs=[pl.BlockSpec((height, block), lambda j: (0, j)) for height, _ in parts * 2],
        out_shape=[jax.ShapeDtypeStruct((height, total), kind) for height, kind in parts * 2],
        compiler_params=params("arbitrary"),
        name="fold_sums",
    )(*firsts, *seconds)
    return outs[:SIDE], outs[SIDE:]


def pack_kernel(groups, experts, capacity, *refs):
    side = SIDE
    out_ref = refs[-1]
    halves = []
    for which in range(2):
        own, others = refs[which * side], refs[which * side + 1 : (which + 1) * side]
        half = own.shape[0]
        value = own[...]
        for other in others:
            code = from_i16(other[half:, :])[0:1]
            value = value + from_i16(other[:half, :]) * down_scale(code)
        halves.append(value)
    values = jnp.concatenate(halves, axis=0)
    columns = values.shape[0]
    span = groups * capacity
    for g in range(groups):
        value = jnp.concatenate(
            [values[:, j * span + g * capacity : j * span + (g + 1) * capacity] for j in range(experts)],
            axis=1,
        )
        coded, code = encode(value)
        out_ref[g, :columns, :] = coded
        out_ref[g, columns:, :] = meta_rows([code])


def pack(firsts, seconds, groups, experts, capacity):
    columns = 2 * firsts[0].shape[0]
    return pl.pallas_call(
        lambda *refs: pack_kernel(groups, experts, capacity, *refs),
        out_shape=jax.ShapeDtypeStruct((groups, columns + 16, experts * capacity), i16),
        compiler_params=params(),
        name="pack_result",
    )(*firsts, *seconds)


def step_to(dx, dy):
    side = SIDE
    return [
        (x * side + y, (x + dx) % side * side + (y + dy) % side)
        for x in range(side)
        for y in range(side)
    ]


def exchange(parts, along_x, sign=1):
    return [parts[0]] + [
        lax.ppermute(parts[r], "width", step_to(sign * r, 0) if along_x else step_to(0, sign * r))
        for r in range(1, SIDE)
    ]


def unpack_kernel(coded_ref, target_ref, *rest):
    own, others, out_ref = rest[0], rest[1:SIDE], rest[SIDE]
    groups, height, slots = coded_ref.shape
    columns, tokens = out_ref.shape
    target = target_ref[...]
    value = jnp.zeros((2 * columns, tokens), f32)
    for g in range(groups):
        part = from_i16(coded_ref[g])
        terms = split(part[:columns] * down_scale(part[columns : columns + 1]))
        place = lax.broadcasted_iota(i32, (slots, tokens), 0) + g * slots
        chosen = (place == target).astype(f32).astype(bf16)
        value = value + jnp.dot(jnp.concatenate(terms, axis=0), chosen, preferred_element_type=f32)
    base = own[...]
    for other in others:
        base = base + from_i16(other[:columns, :]) * down_scale(from_i16(other[columns:, :])[0:1])
    out_ref[...] = value[:columns] + value[columns:] - base


def unpack(coded, target, base_parts):
    groups, height, slots = coded.shape
    return pl.pallas_call(
        unpack_kernel,
        out_shape=jax.ShapeDtypeStruct((height - 16, target.shape[1]), f32),
        compiler_params=params(),
        name="unpack_result",
    )(coded, target, *base_parts)


def send(part, along_x, distance):
    return lax.ppermute(part, "width", step_to(distance, 0) if along_x else step_to(0, distance))


def to_near(parts, along_x):
    own, ahead, behind = parts
    return [own, send(ahead, along_x, 1), send(behind, along_x, -1)]


def local(up_weights, fisher, factor_left, factor_right, calib_rows, routes):
    exp_local, width_rows, hidden = up_weights.shape
    groups = lax.axis_size("expert")
    expert_total = exp_local * groups
    capacity = 2 * calib_rows.shape[0] // expert_total

    index = lax.axis_index("width")
    place = jnp.stack([index // SIDE, index % SIDE]).astype(i32)

    rows_along_x = exchange([calib_rows] * SIDE, True)
    target, outgoing = route(routes, calib_rows, expert_total, capacity)
    incoming = lax.all_to_all(
        outgoing.reshape(groups, exp_local * capacity, width_rows), "expert", 0, 0, tiled=True
    )
    sums = exchange(weighted(place, up_weights, fisher), True)
    incoming, sums = lax.optimization_barrier((incoming, sums))
    near = [rows_along_x[r] for r in (1, SIDE - 1)]
    sums, near = lax.optimization_barrier((sums, near))
    rows_along_x[1], rows_along_x[SIDE - 1] = near
    parts = product(
        place,
        up_weights,
        factor_left,
        factor_right,
        incoming.reshape(groups, exp_local, capacity, width_rows),
    )
    parts, rows_along_x[2] = lax.optimization_barrier((parts, rows_along_x[2]))
    height, span = width_rows // groups, hidden // SIDE + META
    sums = jnp.stack([part.reshape(groups, height, span) for part in sums], axis=1)
    sums = lax.all_to_all(
        sums.reshape(groups, SIDE * height, span), "expert", 0, 0, tiled=True
    )
    legs = []
    for along_x, part in ((True, parts[:SIDE]), (False, parts[SIDE:])):
        middle = part[2].shape[1] // 2
        legs.append(
            [
                part[1],
                send(part[2][:, :middle], along_x, 1),
                part[3],
                send(part[2][:, middle:], along_x, -1),
            ]
        )
    merged = merge(*legs)
    firsts, seconds = [parts[0], *merged[:2]], [parts[SIDE], *merged[2:]]
    coded_base = base_slice(sums)
    coded_base, firsts, seconds = lax.optimization_barrier((coded_base, firsts, seconds))
    firsts, seconds = to_near(firsts, True), to_near(seconds, False)
    coded_base = lax.all_gather(coded_base, "expert", tiled=True)
    coded_base = coded_base.reshape(groups, SIDE, height, span)
    coded_base, firsts, seconds = lax.optimization_barrier((coded_base, firsts, seconds))
    firsts, seconds = fold(firsts, seconds)
    base_parts = base_product(place, coded_base, rows_along_x)
    firsts, seconds = exchange(firsts, False), exchange(seconds, True)
    firsts[0], base_parts = lax.optimization_barrier((firsts[0], base_parts))
    base_parts = exchange(base_parts, False)
    values = pack(firsts, seconds, groups, exp_local, capacity)
    returned = lax.all_to_all(values, "expert", 0, 0, tiled=True)
    chunks = [coded_base[:, r].reshape(width_rows, span) for r in range(SIDE)]
    shared_base = shared(place, exchange(chunks, True, -1))
    return shared_base, unpack(returned, target, base_parts).T


def solution(mesh):
    placed = (
        P("expert", "width", None),
        P("expert", "width"),
        P("expert", "width", None),
        P("expert", None, None),
        P("expert", "width"),
        P("expert", None),
    )
    return jax.shard_map(
        local,
        mesh=mesh,
        in_specs=placed,
        out_specs=(P("width", None), P("expert", "width")),
        check_vma=False,
    )
```

```python
import jax
import jax.numpy as jnp
from jax import lax
from jax.experimental import pallas as pl
from jax.experimental.pallas import tpu as pltpu
from jax.sharding import PartitionSpec as P

f32, bf16, i16, i32 = jnp.float32, jnp.bfloat16, jnp.int16, jnp.int32
VMEM_LIMIT = 48 * 1024 * 1024
TOP = 32000.0
STEPS = 64.0
META = 128
SIDE = 4


def scale_code(biggest):
    return jnp.ceil(jnp.log2(jnp.maximum(biggest, 2.0**-100)) * STEPS) + 1.0


def up_scale(code):
    return jnp.exp2(code * (-1.0 / STEPS)) * TOP


def down_scale(code):
    return jnp.exp2(code * (1.0 / STEPS)) * (1.0 / TOP)


def to_i16(x):
    return jnp.round(x).astype(i32).astype(i16)


def from_i16(x):
    return x.astype(i32).astype(f32)


def params(*semantics):
    return pltpu.CompilerParams(dimension_semantics=semantics or None, vmem_limit_bytes=VMEM_LIMIT)


def weighted_kernel(place_ref, up_ref, fisher_ref, *outs):
    experts, rows, hidden = up_ref.shape
    block = hidden // SIDE
    total = fisher_ref[:, 0:1]
    for j in range(1, experts):
        total = total + fisher_ref[:, j : j + 1]
    fixed = jnp.round(total * 2.0**20).astype(i32)
    lane = lax.broadcasted_iota(i32, (rows, META), 1)
    fixed = jnp.where(lane < 64, fixed >> 15, fixed & 32767)
    for r in range(SIDE):
        part = pl.ds(pl.multiple_of(lax.rem(place_ref[0] + r, SIDE) * block, META), block)
        value = fisher_ref[:, 0:1] * up_ref[0, :, part]
        for j in range(1, experts):
            value = value + fisher_ref[:, j : j + 1] * up_ref[j, :, part]
        code = scale_code(jnp.max(jnp.abs(value), axis=1, keepdims=True))
        outs[r][:, :block] = to_i16(value * up_scale(code))
        outs[r][:, block:] = jnp.where(lane < 32, code.astype(i32), fixed).astype(i16)


def weighted(place, up_weights, fisher):
    experts, rows, hidden = up_weights.shape
    block = 64
    width = hidden // SIDE + META
    return pl.pallas_call(
        weighted_kernel,
        grid=(rows // block,),
        in_specs=[
            pl.BlockSpec(memory_space=pltpu.SMEM),
            pl.BlockSpec((experts, block, hidden), lambda i: (0, i, 0)),
            pl.BlockSpec((block, experts), lambda i: (i, 0)),
        ],
        out_specs=[pl.BlockSpec((block, width), lambda i: (i, 0))] * SIDE,
        out_shape=[jax.ShapeDtypeStruct((rows, width), i16)] * SIDE,
        compiler_params=params("arbitrary"),
        cost_estimate=pl.CostEstimate(
            flops=2 * up_weights.size, bytes_accessed=4 * up_weights.size, transcendentals=0
        ),
        name="weighted_sum",
    )(place, up_weights, fisher.T)


def base_kernel(parts_ref, out_ref):
    groups, rows, width = parts_ref.shape
    hidden = width - META
    value = jnp.zeros((rows, hidden), f32)
    total = jnp.zeros((rows, 1), f32)
    for g in range(groups):
        part = from_i16(parts_ref[g])
        value = value + part[:, :hidden] * down_scale(part[:, hidden : hidden + 1])
        total = total + (part[:, hidden + 32 : hidden + 33] * 32768.0 + part[:, hidden + 64 : hidden + 65])
    base = value * (2.0**20 / total)
    code = scale_code(jnp.max(jnp.abs(base), axis=1, keepdims=True))
    out_ref[:, :hidden] = to_i16(base * up_scale(code))
    out_ref[:, hidden:] = jnp.broadcast_to(code.astype(i32), (rows, META)).astype(i16)


def base_slice(parts):
    groups, rows, width = parts.shape
    return pl.pallas_call(
        base_kernel,
        out_shape=jax.ShapeDtypeStruct((rows, width), i16),
        compiler_params=params(),
        name="base_slice",
    )(parts)


def decode_rows(coded):
    block = coded.shape[1] - META
    return from_i16(coded[:, :block]) * down_scale(from_i16(coded[:, block:])[:, 0:1])


def shared_kernel(place_ref, *refs):
    out_ref = refs[-1]
    block = out_ref.shape[1] // SIDE
    for r in range(SIDE):
        start = pl.multiple_of(lax.rem(place_ref[0] + r, SIDE) * block, META)
        out_ref[:, pl.ds(start, block)] = decode_rows(refs[r][...])


def shared(place, codeds):
    rows, width = codeds[0].shape
    vmem = pl.BlockSpec(memory_space=pltpu.VMEM)
    return pl.pallas_call(
        shared_kernel,
        in_specs=[pl.BlockSpec(memory_space=pltpu.SMEM)] + [vmem] * SIDE,
        out_shape=jax.ShapeDtypeStruct((rows, (width - META) * SIDE), f32),
        compiler_params=params(),
        name="shared_base",
    )(place, *codeds)


def route_kernel(experts, capacity, routes_ref, rows_ref, target_ref, out_ref):
    tokens = rows_ref.shape[0]
    block = out_ref.shape[0]
    step = pl.program_id(0)

    @pl.when(step == 0)
    def _():
        routes = routes_ref[...]
        hit = lax.broadcasted_iota(i32, (experts, tokens), 0) == routes
        one_hot = hit.astype(f32).astype(bf16)
        before = lax.broadcasted_iota(i32, (tokens, tokens), 0) < lax.broadcasted_iota(
            i32, (tokens, tokens), 1
        )
        earlier = jnp.dot(one_hot, before.astype(f32).astype(bf16), preferred_element_type=f32)
        slot = jnp.sum(jnp.where(hit, earlier, 0.0), axis=0, keepdims=True)
        target_ref[...] = routes * capacity + slot.astype(i32)

    place = lax.broadcasted_iota(i32, (block, tokens), 0) + step * block
    chosen = (place == target_ref[...]).astype(f32).astype(bf16)
    out_ref[...] = jnp.dot(chosen, rows_ref[...], preferred_element_type=f32).astype(bf16)


def route(routes, calib_rows, experts, capacity):
    tokens, width = calib_rows.shape
    slots = experts * capacity
    block = 256
    return pl.pallas_call(
        lambda *refs: route_kernel(experts, capacity, *refs),
        grid=(slots // block,),
        in_specs=[
            pl.BlockSpec((1, tokens), lambda i: (0, 0)),
            pl.BlockSpec((tokens, width), lambda i: (0, 0)),
        ],
        out_specs=[
            pl.BlockSpec((1, tokens), lambda i: (0, 0)),
            pl.BlockSpec((block, width), lambda i: (i, 0)),
        ],
        out_shape=[
            jax.ShapeDtypeStruct((1, tokens), i32),
            jax.ShapeDtypeStruct((slots, width), bf16),
        ],
        compiler_params=params("arbitrary"),
        cost_estimate=pl.CostEstimate(
            flops=2 * slots * tokens * width, bytes_accessed=4 * slots * width, transcendentals=0
        ),
        name="route_rows",
    )(routes.reshape(1, tokens), calib_rows)


def meta_rows(codes):
    lanes = codes[0].shape[1]
    row = lax.broadcasted_iota(i32, (16, lanes), 0)
    meta = jnp.zeros((16, lanes), i32)
    for position, code in enumerate(codes):
        meta = jnp.where(row == position, code.astype(i32), meta)
    return meta.astype(i16)


def split(value):
    high = value.astype(bf16)
    return high, (value - high.astype(f32)).astype(bf16)


def encode(value):
    code = scale_code(jnp.max(jnp.abs(value), axis=0, keepdims=True))
    return to_i16(value * up_scale(code)), code


def product_kernel(place_ref, up_ref, left_ref, right_ref, rows_ref, *rest):
    side = SIDE
    firsts, seconds, held = rest[:side], rest[side : 2 * side], rest[2 * side]
    _, width, hidden = up_ref.shape
    block = hidden // side
    columns = block // side
    half = columns // 2

    groups, _, capacity, _ = rows_ref.shape
    rows = rows_ref[:, 0].reshape(groups * capacity, width)
    twice = jnp.concatenate([rows, rows], axis=1)
    contract = (((0,), (1,)), ((), ()))
    second_codes = [[] for s in range(side)]
    left_high, left_low = split(left_ref[0])
    left_all = jnp.concatenate([left_high, left_low], axis=1)
    for r in range(side):
        part = pl.ds(pl.multiple_of(lax.rem(place_ref[0] + r, side) * block, block), block)
        right_high, right_low = split(right_ref[0, :, part])
        low_rank = jnp.dot(
            left_all, jnp.concatenate([right_high] * 2, axis=0), preferred_element_type=f32
        ) + jnp.dot(left_high, right_low, preferred_element_type=f32)
        high, low = split(up_ref[0, :, part] - low_rank)
        held[r] = lax.dot_general(
            jnp.concatenate([high, low], axis=0), twice, contract, preferred_element_type=f32
        )
        first_codes = []
        for s in range(side):
            start = lax.rem(place_ref[1] + s, side) * columns
            first = held[r, pl.ds(pl.multiple_of(start, 8), half), :]
            second = held[r, pl.ds(pl.multiple_of(start + half, 8), half), :]
            if r == 0:
                firsts[0][s * half : (s + 1) * half, :] = first
            else:
                coded, code = encode(first)
                firsts[r][s * half : (s + 1) * half, :] = coded
                first_codes.append(code)
            if s == 0:
                seconds[0][r * half : (r + 1) * half, :] = second
            else:
                coded, code = encode(second)
                seconds[s][r * half : (r + 1) * half, :] = coded
                second_codes[s].append(code)
        if r > 0:
            firsts[r][side * half :, :] = meta_rows(first_codes)
    for s in range(1, side):
        seconds[s][side * half :, :] = meta_rows(second_codes[s])


def product(place, up_weights, factor_left, factor_right, routed):
    experts, width, hidden = up_weights.shape
    rank = factor_left.shape[2]
    groups, _, capacity, _ = routed.shape
    rows = groups * capacity
    own = hidden // SIDE // 2
    parts = [(own, f32)] + [(own + 16, i16)] * (SIDE - 1)
    return pl.pallas_call(
        product_kernel,
        grid=(experts,),
        in_specs=[
            pl.BlockSpec(memory_space=pltpu.SMEM),
            pl.BlockSpec((1, width, hidden), lambda j: (j, 0, 0)),
            pl.BlockSpec((1, width, rank), lambda j: (j, 0, 0)),
            pl.BlockSpec((1, rank, hidden), lambda j: (j, 0, 0)),
            pl.BlockSpec((groups, 1, capacity, width), lambda j: (0, j, 0, 0)),
        ],
        out_specs=[pl.BlockSpec((height, rows), lambda j: (0, j)) for height, _ in parts * 2],
        out_shape=[jax.ShapeDtypeStruct((height, experts * rows), kind) for height, kind in parts * 2],
        scratch_shapes=[pltpu.VMEM((SIDE, hidden // SIDE, rows), f32)],
        compiler_params=params("arbitrary"),
        cost_estimate=pl.CostEstimate(
            flops=4 * experts * rows * width * hidden,
            bytes_accessed=4 * (up_weights.size + experts * rows * hidden),
            transcendentals=0,
        ),
        name="routed_product",
    )(place, up_weights, factor_left, factor_right, routed)


def base_product_kernel(place_ref, coded_ref, *refs):
    side = SIDE
    rows, outs, held = refs[:side], refs[side : 2 * side], refs[-1]
    groups, _, height, width = coded_ref.shape
    columns = held.shape[0] // side
    contract = (((0,), (1,)), ((), ()))
    value = None
    for r in range(side):
        part = decode_rows(coded_ref[:, r].reshape(groups * height, width))
        for term in split(part):
            added = lax.dot_general(term, rows[r][...], contract, preferred_element_type=f32)
            value = added if value is None else value + added
    held[...] = value
    for s in range(side):
        start = pl.multiple_of(lax.rem(place_ref[1] + s, side) * columns, 8)
        piece = held[pl.ds(start, columns), :]
        if s == 0:
            outs[0][...] = piece
        else:
            coded, code = encode(piece)
            outs[s][:columns, :] = coded
            outs[s][columns:, :] = meta_rows([code])


def base_product(place, coded, rows):
    groups, side, height, width = coded.shape
    tokens = rows[0].shape[0]
    block = width - META
    columns = block // side
    vmem = pl.BlockSpec(memory_space=pltpu.VMEM)
    return pl.pallas_call(
        base_product_kernel,
        in_specs=[pl.BlockSpec(memory_space=pltpu.SMEM)] + [vmem] * (side + 1),
        out_shape=[jax.ShapeDtypeStruct((columns, tokens), f32)]
        + [jax.ShapeDtypeStruct((columns + 16, tokens), i16)] * (side - 1),
        scratch_shapes=[pltpu.VMEM((block, tokens), f32)],
        compiler_params=params(),
        cost_estimate=pl.CostEstimate(
            flops=4 * groups * side * height * tokens * block,
            bytes_accessed=4 * groups * side * height * block,
            transcendentals=0,
        ),
        name="base_product",
    )(place, coded, *rows)


def merge_kernel(*refs):
    outs = refs[-4:]
    for which in range(4):
        coded, passed, out_ref = refs[2 * which], refs[2 * which + 1], outs[which]
        half = (coded.shape[0] - 16) // SIDE
        lanes = passed.shape[1]
        start = (which % 2) * lanes
        here, there = slice(start, start + lanes), slice(lanes - start, 2 * lanes - start)
        out_ref[:, there] = coded[:, there]
        own_codes, passed_codes = from_i16(coded[SIDE * half :, here]), from_i16(passed[SIDE * half :, :])
        codes = []
        for s in range(SIDE):
            piece = slice(s * half, (s + 1) * half)
            value = from_i16(coded[piece, here]) * down_scale(own_codes[s : s + 1])
            value = value + from_i16(passed[piece, :]) * down_scale(passed_codes[s : s + 1])
            summed, code = encode(value)
            out_ref[piece, here] = summed
            codes.append(code)
        out_ref[SIDE * half :, here] = meta_rows(codes)


def merge(first, second):
    operands = [*first, *second]
    shape = operands[0].shape
    return pl.pallas_call(
        merge_kernel,
        out_shape=[jax.ShapeDtypeStruct(shape, i16)] * 4,
        compiler_params=params(),
        name="merge_parts",
    )(*operands)


def fold_kernel(*refs):
    side, given = SIDE, 3
    for which in range(2):
        own, others = refs[which * given], refs[which * given + 1 : (which + 1) * given]
        outs = refs[2 * given + which * side : 2 * given + (which + 1) * side]
        half = own.shape[0] // side
        for s in range(side):
            piece = slice(s * half, (s + 1) * half)
            value = own[piece, :]
            for other in others:
                code = from_i16(other[side * half :, :])[s : s + 1]
                value = value + from_i16(other[piece, :]) * down_scale(code)
            if s == 0:
                outs[0][...] = value
            else:
                coded, code = encode(value)
                outs[s][:half, :] = coded
                outs[s][half:, :] = meta_rows([code])


def fold(firsts, seconds):
    own, total = firsts[0].shape
    half = own // SIDE
    block = 512
    heights = [own] + [own + 16] * 2
    parts = [(half, f32)] + [(half + 16, i16)] * (SIDE - 1)
    outs = pl.pallas_call(
        fold_kernel,
        grid=(total // block,),
        in_specs=[pl.BlockSpec((height, block), lambda j: (0, j)) for height in heights * 2],
        out_specs=[pl.BlockSpec((height, block), lambda j: (0, j)) for height, _ in parts * 2],
        out_shape=[jax.ShapeDtypeStruct((height, total), kind) for height, kind in parts * 2],
        compiler_params=params("arbitrary"),
        name="fold_sums",
    )(*firsts, *seconds)
    return outs[:SIDE], outs[SIDE:]


def pack_kernel(groups, experts, capacity, *refs):
    side = SIDE
    out_ref = refs[-1]
    halves = []
    for which in range(2):
        own, others = refs[which * side], refs[which * side + 1 : (which + 1) * side]
        half = own.shape[0]
        value = own[...]
        for other in others:
            code = from_i16(other[half:, :])[0:1]
            value = value + from_i16(other[:half, :]) * down_scale(code)
        halves.append(value)
    values = jnp.concatenate(halves, axis=0)
    columns = values.shape[0]
    span = groups * capacity
    for g in range(groups):
        value = jnp.concatenate(
            [values[:, j * span + g * capacity : j * span + (g + 1) * capacity] for j in range(experts)],
            axis=1,
        )
        coded, code = encode(value)
        out_ref[g, :columns, :] = coded
        out_ref[g, columns:, :] = meta_rows([code])


def pack(firsts, seconds, groups, experts, capacity):
    columns = 2 * firsts[0].shape[0]
    return pl.pallas_call(
        lambda *refs: pack_kernel(groups, experts, capacity, *refs),
        out_shape=jax.ShapeDtypeStruct((groups, columns + 16, experts * capacity), i16),
        compiler_params=params(),
        name="pack_result",
    )(*firsts, *seconds)


def step_to(dx, dy):
    side = SIDE
    return [
        (x * side + y, (x + dx) % side * side + (y + dy) % side)
        for x in range(side)
        for y in range(side)
    ]


def exchange(parts, along_x, sign=1):
    return [parts[0]] + [
        lax.ppermute(parts[r], "width", step_to(sign * r, 0) if along_x else step_to(0, sign * r))
        for r in range(1, SIDE)
    ]


def unpack_kernel(coded_ref, target_ref, *rest):
    own, others, out_ref = rest[0], rest[1:SIDE], rest[SIDE]
    groups, height, slots = coded_ref.shape
    columns, tokens = out_ref.shape
    target = target_ref[...]
    value = jnp.zeros((2 * columns, tokens), f32)
    for g in range(groups):
        part = from_i16(coded_ref[g])
        terms = split(part[:columns] * down_scale(part[columns : columns + 1]))
        place = lax.broadcasted_iota(i32, (slots, tokens), 0) + g * slots
        chosen = (place == target).astype(f32).astype(bf16)
        value = value + jnp.dot(jnp.concatenate(terms, axis=0), chosen, preferred_element_type=f32)
    base = own[...]
    for other in others:
        base = base + from_i16(other[:columns, :]) * down_scale(from_i16(other[columns:, :])[0:1])
    out_ref[...] = value[:columns] + value[columns:] - base


def unpack(coded, target, base_parts):
    groups, height, slots = coded.shape
    return pl.pallas_call(
        unpack_kernel,
        out_shape=jax.ShapeDtypeStruct((height - 16, target.shape[1]), f32),
        compiler_params=params(),
        name="unpack_result",
    )(coded, target, *base_parts)


def send(part, along_x, distance):
    return lax.ppermute(part, "width", step_to(distance, 0) if along_x else step_to(0, distance))


def to_near(parts, along_x):
    own, ahead, behind = parts
    return [own, send(ahead, along_x, 1), send(behind, along_x, -1)]


def local(up_weights, fisher, factor_left, factor_right, calib_rows, routes):
    exp_local, width_rows, hidden = up_weights.shape
    groups = lax.axis_size("expert")
    expert_total = exp_local * groups
    capacity = 2 * calib_rows.shape[0] // expert_total

    index = lax.axis_index("width")
    place = jnp.stack([index // SIDE, index % SIDE]).astype(i32)

    rows_along_x = exchange([calib_rows] * SIDE, True)
    target, outgoing = route(routes, calib_rows, expert_total, capacity)
    incoming = lax.all_to_all(
        outgoing.reshape(groups, exp_local * capacity, width_rows), "expert", 0, 0, tiled=True
    )
    sums = exchange(weighted(place, up_weights, fisher), True)
    incoming, sums = lax.optimization_barrier((incoming, sums))
    near = [rows_along_x[r] for r in (1, SIDE - 1)]
    sums, near = lax.optimization_barrier((sums, near))
    rows_along_x[1], rows_along_x[SIDE - 1] = near
    parts = product(
        place,
        up_weights,
        factor_left,
        factor_right,
        incoming.reshape(groups, exp_local, capacity, width_rows),
    )
    parts, rows_along_x[2] = lax.optimization_barrier((parts, rows_along_x[2]))
    height, span = width_rows // groups, hidden // SIDE + META
    sums = jnp.stack([part.reshape(groups, height, span) for part in sums], axis=1)
    sums = lax.all_to_all(
        sums.reshape(groups, SIDE * height, span), "expert", 0, 0, tiled=True
    )
    legs = []
    for along_x, part in ((True, parts[:SIDE]), (False, parts[SIDE:])):
        middle = part[2].shape[1] // 2
        legs.append(
            [
                part[1],
                send(part[2][:, :middle], along_x, 1),
                part[3],
                send(part[2][:, middle:], along_x, -1),
            ]
        )
    merged = merge(*legs)
    firsts, seconds = [parts[0], *merged[:2]], [parts[SIDE], *merged[2:]]
    coded_base = base_slice(sums)
    coded_base, firsts, seconds = lax.optimization_barrier((coded_base, firsts, seconds))
    firsts, seconds = to_near(firsts, True), to_near(seconds, False)
    coded_base = lax.all_gather(coded_base, "expert", tiled=True)
    coded_base = coded_base.reshape(groups, SIDE, height, span)
    coded_base, firsts, seconds = lax.optimization_barrier((coded_base, firsts, seconds))
    firsts, seconds = fold(firsts, seconds)
    base_parts = base_product(place, coded_base, rows_along_x)
    firsts, seconds = exchange(firsts, False), exchange(seconds, True)
    firsts[0], base_parts = lax.optimization_barrier((firsts[0], base_parts))
    base_parts = exchange(base_parts, False)
    values = pack(firsts, seconds, groups, exp_local, capacity)
    returned = lax.all_to_all(values, "expert", 0, 0, tiled=True)
    chunks = [coded_base[:, r].reshape(width_rows, span) for r in range(SIDE)]
    shared_base = shared(place, exchange(chunks, True, -1))
    return shared_base, unpack(returned, target, base_parts).T


def solution(mesh):
    placed = (
        P("expert", "width", None),
        P("expert", "width"),
        P("expert", "width", None),
        P("expert", None, None),
        P("expert", "width"),
        P("expert", None),
    )
    return jax.shard_map(
        local,
        mesh=mesh,
        in_specs=placed,
        out_specs=(P("width", None), P("expert", "width")),
        check_vma=False,
    )
```
